128 devices in a mesh: resp: 16 (over z, x_hi, core), tp: 8 (over x_lo, y).
Axes of the slice: x: 4 (x_hi: 2, x_lo: 2; x = x_hi * 2 + x_lo), y: 4, z: 4, core: 2. Of those that a mesh axis runs over, the one named last changes fastest.
Arguments:
- queries: bfloat16 [16, 512, 5120], P('resp', None, 'tp'), may hold values from -5 to 5
- response_keys: bfloat16 [16, 512, 1024], P('resp', None, 'tp'), may hold values from -5 to 5
- response_values: bfloat16 [16, 512, 1024], P('resp', None, 'tp'), may hold values from -5 to 5
- prompt_key_rows: bfloat16 [1024, 1024], P('resp', 'tp'), may hold values from -5 to 5
- prompt_value_rows: bfloat16 [1024, 1024], P('resp', 'tp'), may hold values from -5 to 5
- upstream: bfloat16 [16, 512, 5120], P('resp', 'tp'), may hold values from -6 to 6
- lengths: int32 [16], P('resp'), may hold values from 128 to 512, as said below
- query_weight: bfloat16 [5120, 5120], P(None, 'tp'), may hold values from -0.078125 to 0.078125
- key_matrix: bfloat16 [5120, 1024], P(None, 'tp'), may hold values from -0.078125 to 0.078125
- value_matrix: bfloat16 [5120, 1024], P(None, 'tp'), may hold values from -0.078125 to 0.078125
- out_weight: bfloat16 [5120, 5120], P('tp'), may hold values from -2.5 to 2.5
Outputs:
- input_grad: bfloat16 [16, 512, 5120], P('resp', 'tp')
- prompt_key_gradient: float32 [1024, 1024], P('resp', 'tp')
- prompt_value_gradient: float32 [1024, 1024], P('resp', 'tp')
The draws below stay inside these ranges and needn't reach their ends.
Inputs may be any that keep to these rules, and one draw needn't show every extreme that they name: `lengths`: one response of each draw has exactly 512 live tokens.
All inputs are finite; a program needn't handle non-finite values.
Results may differ from the reference program's by a relative error of at most 0.018.
Values may be sent and summed in bfloat16 or wider, within the bound.
A program may use at most 128 MiB of HBM per device.

```python
import math
import jax
import jax.numpy as jnp
from jax import lax

MODEL_WIDTH = 5120
QUERY_HEAD_COUNT = 40
KEY_VALUE_HEADS = 8
HEAD_WIDTH = 128
RESPONSE_SLOTS = 512
SAMPLE_COUNT = 16
PROMPT_TOKENS = 1024
N_TP = 8


def draw_queries(key, part):
    key = jax.random.fold_in(key, 3)
    value_rows_all = jnp.clip(jax.random.normal(key, (SAMPLE_COUNT, RESPONSE_SLOTS, QUERY_HEAD_COUNT, HEAD_WIDTH), jnp.float32), -5.0, 5.0)
    return value_rows_all.reshape(SAMPLE_COUNT, RESPONSE_SLOTS, QUERY_HEAD_COUNT * HEAD_WIDTH).astype(jnp.bfloat16)


def draw_prompt_key_rows(key, part):
    key = jax.random.fold_in(key, 7)
    value_rows_all = jnp.clip(jax.random.normal(key, (PROMPT_TOKENS, KEY_VALUE_HEADS, HEAD_WIDTH), jnp.float32), -5.0, 5.0)
    return value_rows_all.reshape(PROMPT_TOKENS, KEY_VALUE_HEADS * HEAD_WIDTH).astype(jnp.bfloat16)


def draw_lengths(key, part):
    key = jax.random.fold_in(key, 5)
    length_key = jax.random.fold_in(key, 1)
    which_key = jax.random.fold_in(key, 2)
    drawn = jax.random.randint(length_key, (SAMPLE_COUNT,), RESPONSE_SLOTS // 4, RESPONSE_SLOTS + 1)
    longest = jax.random.randint(which_key, (), 0, SAMPLE_COUNT)
    return jnp.where(jnp.arange(SAMPLE_COUNT, dtype=jnp.int32) == longest, RESPONSE_SLOTS, drawn).astype(jnp.int32)


def steps_of(rng, extent, pieces, low, top_value):
    def one(axis_at, blocks):
        draws = jax.random.uniform(jax.random.fold_in(jax.random.fold_in(rng, 6), axis_at), (blocks,), jnp.float32, low / len(pieces), top_value / len(pieces))
        return jnp.repeat(jnp.exp(draws), extent[axis_at] // blocks).reshape((-1,) + (1,) * (len(extent) - axis_at - 1))

    level = one(*pieces[0])
    for cut in pieces[1:]:
        level = level * one(*cut)
    return level


def noise(key, shape, width, reach, cuts=(), held_as=jnp.bfloat16):
    entries = width * jax.random.normal(key, shape, jnp.float32)
    if cuts:
        entries = entries * steps_of(key, shape, cuts, -0.22, 0.18)
    return jnp.clip(entries, -reach, reach).astype(held_as)


def setup_inputs(seed: int = 0) -> dict:
    streams_of = jax.random.split(jax.random.key(seed), 12)
    return {
        "queries": draw_queries(jax.random.fold_in(streams_of[11], 71), 0),
        "response_keys": noise(streams_of[1], (SAMPLE_COUNT, RESPONSE_SLOTS, KEY_VALUE_HEADS * HEAD_WIDTH), 1.0, 5.0, ((0, 16), (2, 8))),
        "response_values": noise(streams_of[2], (SAMPLE_COUNT, RESPONSE_SLOTS, KEY_VALUE_HEADS * HEAD_WIDTH), 1.0, 5.0, ((0, 16), (2, 8))),
        "prompt_key_rows": draw_prompt_key_rows(jax.random.fold_in(streams_of[11], 71), 0),
        "prompt_value_rows": noise(streams_of[4], (PROMPT_TOKENS, KEY_VALUE_HEADS * HEAD_WIDTH), 1.0, 5.0, ((0, 16), (1, 8))),
        "upstream": noise(streams_of[5], (SAMPLE_COUNT, RESPONSE_SLOTS, MODEL_WIDTH), 1.0, 6.0, ((0, 16), (1, 8))),
        "lengths": draw_lengths(jax.random.fold_in(streams_of[11], 71), 0),
        "query_weight": noise(streams_of[7], (MODEL_WIDTH, QUERY_HEAD_COUNT * HEAD_WIDTH), (QUERY_HEAD_COUNT * HEAD_WIDTH) ** -0.5, 0.078125, ((1, 8),)),
        "key_matrix": noise(streams_of[8], (MODEL_WIDTH, KEY_VALUE_HEADS * HEAD_WIDTH), (QUERY_HEAD_COUNT * HEAD_WIDTH) ** -0.5, 0.078125, ((1, 8),)),
        "value_matrix": noise(streams_of[9], (MODEL_WIDTH, KEY_VALUE_HEADS * HEAD_WIDTH), (QUERY_HEAD_COUNT * HEAD_WIDTH) ** -0.5, 0.078125, ((1, 8),)),
        "out_weight": noise(streams_of[10], (QUERY_HEAD_COUNT * HEAD_WIDTH, MODEL_WIDTH), (max(MODEL_WIDTH // 1024, 1)) ** -0.5, 2.5, ((0, 8),)),
    }


def head_backward(query_head, grad_head, all_keys, all_values, scaling):
    row_total = query_head.shape[0]
    key_total = all_keys.shape[0]
    prompt_len = key_total - row_total
    scores = jnp.dot(query_head, all_keys.T, preferred_element_type=jnp.float32) * scaling
    positions = jnp.arange(row_total, dtype=jnp.int32)[:, None]
    key_index = jnp.arange(key_total, dtype=jnp.int32)[None, :]
    visible = (key_index < prompt_len) | (key_index - prompt_len <= positions)
    scores = jnp.where(visible, scores, -jnp.inf)
    row_max = lax.optimization_barrier(jnp.max(scores, axis=1, keepdims=True))
    exponent = jnp.exp(scores - row_max)
    probability = exponent / lax.optimization_barrier(jnp.sum(exponent, axis=1, keepdims=True))
    probability_b = probability.astype(jnp.bfloat16)
    grad_prob = jnp.dot(grad_head, all_values.T, preferred_element_type=jnp.float32)
    row_delta = lax.optimization_barrier(jnp.sum(probability * grad_prob, axis=1, keepdims=True))
    grad_score = (probability * (grad_prob - row_delta) * scaling).astype(jnp.bfloat16)
    query_gradient = jnp.dot(grad_score, all_keys, preferred_element_type=jnp.float32).astype(jnp.bfloat16)
    key_term = jnp.dot(grad_score.T, query_head, preferred_element_type=jnp.float32)
    value_term = jnp.dot(probability_b.T, grad_head, preferred_element_type=jnp.float32)
    return (query_gradient, key_term, value_term)

def reference(queries, response_keys, response_values, prompt_key_rows, prompt_value_rows, upstream, lengths, query_weight, key_matrix, value_matrix, out_weight):
    sample_count = QUERY_HEAD_COUNT // KEY_VALUE_HEADS
    scaling = 1.0 / math.sqrt(HEAD_WIDTH)
    heads_dev = QUERY_HEAD_COUNT // N_TP
    key_value_heads_local = KEY_VALUE_HEADS // N_TP
    prompt_keys_3 = prompt_key_rows.reshape(PROMPT_TOKENS, KEY_VALUE_HEADS, HEAD_WIDTH)
    prompt_values_3 = prompt_value_rows.reshape(PROMPT_TOKENS, KEY_VALUE_HEADS, HEAD_WIDTH)

    def one_response(response_index):
        positions = jnp.arange(RESPONSE_SLOTS, dtype=jnp.int32)
        live = positions < lengths[response_index]
        masked = jnp.where(live[:, None], upstream[response_index], jnp.zeros((), jnp.bfloat16))
        grad_out = jnp.dot(masked, out_weight.T, preferred_element_type=jnp.float32).astype(jnp.bfloat16)
        query_heads = queries[response_index].reshape(RESPONSE_SLOTS, QUERY_HEAD_COUNT, HEAD_WIDTH)
        grad_heads = grad_out.reshape(RESPONSE_SLOTS, QUERY_HEAD_COUNT, HEAD_WIDTH)
        response_own_keys = response_keys[response_index].reshape(RESPONSE_SLOTS, KEY_VALUE_HEADS, HEAD_WIDTH)
        response_own_values = response_values[response_index].reshape(RESPONSE_SLOTS, KEY_VALUE_HEADS, HEAD_WIDTH)

        def head_of_keys(pair_index):
            all_keys = jnp.concatenate([prompt_keys_3[:, pair_index], response_own_keys[:, pair_index]], axis=0)
            all_values = jnp.concatenate([prompt_values_3[:, pair_index], response_own_values[:, pair_index]], axis=0)

            def one_head(member):
                head_index = pair_index * sample_count + member
                return head_backward(query_heads[:, head_index], grad_heads[:, head_index], all_keys, all_values, scaling)
            query_gradient, key_term, value_term = lax.map(one_head, jnp.arange(sample_count, dtype=jnp.int32))
            return (query_gradient, lax.optimization_barrier(jnp.sum(key_term, axis=0)), lax.optimization_barrier(jnp.sum(value_term, axis=0)))
        query_gradient, key_gradient, value_gradient = lax.map(head_of_keys, jnp.arange(KEY_VALUE_HEADS, dtype=jnp.int32))
        grad_flat = query_gradient.reshape(QUERY_HEAD_COUNT, RESPONSE_SLOTS, HEAD_WIDTH).transpose(1, 0, 2).reshape(RESPONSE_SLOTS, QUERY_HEAD_COUNT * HEAD_WIDTH)
        response_key_gradient = key_gradient[:, PROMPT_TOKENS:].astype(jnp.bfloat16).transpose(1, 0, 2).reshape(RESPONSE_SLOTS, KEY_VALUE_HEADS * HEAD_WIDTH)
        response_value_gradient = value_gradient[:, PROMPT_TOKENS:].astype(jnp.bfloat16).transpose(1, 0, 2).reshape(RESPONSE_SLOTS, KEY_VALUE_HEADS * HEAD_WIDTH)
        summed = jnp.zeros((RESPONSE_SLOTS, MODEL_WIDTH), jnp.float32)
        for group_index in range(N_TP):
            qcols = slice(group_index * heads_dev * HEAD_WIDTH, (group_index + 1) * heads_dev * HEAD_WIDTH)
            kcols = slice(group_index * key_value_heads_local * HEAD_WIDTH, (group_index + 1) * key_value_heads_local * HEAD_WIDTH)
            term = jnp.dot(grad_flat[:, qcols], query_weight[:, qcols].T, preferred_element_type=jnp.float32)
            term = term + jnp.dot(response_key_gradient[:, kcols], key_matrix[:, kcols].T, preferred_element_type=jnp.float32)
            term = term + jnp.dot(response_value_gradient[:, kcols], value_matrix[:, kcols].T, preferred_element_type=jnp.float32)
            rounded = lax.optimization_barrier(term.astype(jnp.bfloat16))
            summed = summed + rounded.astype(jnp.float32)
        return (summed.astype(jnp.bfloat16), key_gradient[:, :PROMPT_TOKENS], value_gradient[:, :PROMPT_TOKENS])
    input_grad, key_pieces, value_pieces = lax.map(one_response, jnp.arange(SAMPLE_COUNT, dtype=jnp.int32))
    prompt_key_gradient = lax.optimization_barrier(jnp.sum(key_pieces, axis=0)).transpose(1, 0, 2).reshape(PROMPT_TOKENS, KEY_VALUE_HEADS * HEAD_WIDTH)
    prompt_value_gradient = lax.optimization_barrier(jnp.sum(value_pieces, axis=0)).transpose(1, 0, 2).reshape(PROMPT_TOKENS, KEY_VALUE_HEADS * HEAD_WIDTH)
    return (input_grad, prompt_key_gradient, prompt_value_gradient)
```

```python
import functools
import math

import jax
import jax.numpy as jnp
from jax import lax
from jax.experimental import pallas as pl
from jax.experimental.pallas import tpu as pltpu
from jax.sharding import PartitionSpec as P

MESH = pl.DeviceIdType.MESH
BF = jnp.bfloat16
F32 = jnp.float32
WIDTH = 5120
HEADS = 5
HEAD = 128
ROWS = 64
GROUP = 256
CHUNK = 256
LANES = HEADS * GROUP
HALF = WIDTH // 2
QUARTER = WIDTH // 4
NT = (((1,), (1,)), ((), ()))


def dot_nt(a, b):
    return lax.dot_general(a, b, NT, preferred_element_type=F32)


def dot(a, b):
    return jnp.dot(a, b, preferred_element_type=F32)


def kernel(
    len_ref,
    q_hbm,
    rk_hbm,
    rv_hbm,
    pk_hbm,
    pv_hbm,
    up_ref,
    wq_hbm,
    wk_hbm,
    wv_hbm,
    wo_hbm,
    out_ref,
    pkg_ref,
    pvg_ref,
    blocks,
    wo,
    wc,
    q,
    kv,
    kt,
    vt,
    scores,
    prob,
    out_t,
    go_acc,
    go,
    delta,
    ds,
    dq_t,
    dkv,
    grads,
    landed,
    p_send,
    p_land,
    p_land_z,
    p_land_h,
    load_sem,
    gs_sem,
    gr_sem,
    rs_sem,
    rr_sem,
    ps_sem,
    pr_sem,
):
    r = lax.axis_index("resp")
    t = lax.axis_index("tp")
    z, xh, core = r // 4, (r // 2) % 2, r % 2
    xl, y = t // 4, t % 4
    up1, down1, far1 = (y + 1) % 4, (y + 3) % 4, (y + 2) % 4
    ox = 1 - xl
    i_x, i_u, i_d, i_f = ox * 4 + y, xl * 4 + up1, xl * 4 + down1, xl * 4 + far1
    i_xu, i_xd, i_xf = ox * 4 + up1, ox * 4 + down1, ox * 4 + far1
    dev_x, dev_u, dev_d = (r, i_x), (r, i_u), (r, i_d)
    dev_s = (z * 4 + xh * 2 + 1 - core, t)
    dev_h = (z * 4 + (1 - xh) * 2 + core, t)
    dev_z = [(((z + k) % 4) * 4 + xh * 2 + core, t) for k in (1, 2, 3)]

    barrier = pltpu.get_barrier_semaphore()
    peers = [dev_x, dev_u, dev_d, dev_s, dev_h] + dev_z
    for peer in peers:
        pl.semaphore_signal(barrier, inc=1, device_id=peer, device_id_type=MESH)

    loads = []

    def load(src, dst):
        copy = pltpu.make_async_copy(src, dst, load_sem.at[len(loads)])
        copy.start()
        loads.append(copy)
        return copy

    my_slot = core * 8 + z * 2 + xh
    own_prompt = [
        load(pk_hbm, kv.at[my_slot, :, 0:HEAD]),
        load(pv_hbm, kv.at[my_slot, :, HEAD : 2 * HEAD]),
    ]
    own_keys = []
    for i in range(8):
        rows = pl.ds(i * ROWS, ROWS)
        own_keys.append(load(rk_hbm.at[0, rows], kv.at[16 + i, :, 0:HEAD]))
        own_keys.append(load(rv_hbm.at[0, rows], kv.at[16 + i, :, HEAD : 2 * HEAD]))
    own_q = []
    for g in range(2):
        for h in range(HEADS):
            own_q.append(
                load(q_hbm.at[0, pl.ds(g * GROUP, GROUP), pl.ds(h * HEAD, HEAD)], q.at[g, h])
            )

    position = t * ROWS + lax.broadcasted_iota(jnp.int32, (ROWS, WIDTH), 0)
    live = position < len_ref[0]
    blocks[t] = jnp.where(live, up_ref[0], jnp.zeros((), BF))

    pl.semaphore_wait(barrier, len(peers))

    def g_copy(k, slot, rows, dev):
        ref = blocks.at[slot, pl.ds(rows[0], rows[1])]
        return pltpu.make_async_remote_copy(
            src_ref=ref, dst_ref=ref, send_sem=gs_sem.at[k], recv_sem=gr_sem.at[k],
            device_id=dev, device_id_type=MESH,
        )

    def g_wait(k, slot, rows):
        ref = blocks.at[slot, pl.ds(rows[0], rows[1])]
        pltpu.make_async_remote_copy(
            src_ref=ref, dst_ref=ref, send_sem=gs_sem.at[k], recv_sem=gr_sem.at[k],
            device_id=dev_x, device_id_type=MESH,
        ).wait_recv()

    h0, h1, whole = (0, 32), (32, 32), (0, 64)
    q2, q3 = (32, 16), (48, 16)
    sent = []

    def send(k, slot, rows, dev):
        copy = g_copy(k, slot, rows, dev)
        copy.start()
        sent.append(copy)

    send(0, t, whole, dev_x)
    send(1, t, whole, dev_u)
    send(2, t, whole, dev_d)

    def p_copy(k, src, dst, dev):
        return pltpu.make_async_remote_copy(
            src_ref=src, dst_ref=dst, send_sem=ps_sem.at[k], recv_sem=pr_sem.at[k],
            device_id=dev, device_id_type=MESH,
        )

    for copy in own_prompt:
        copy.wait()
    to_h = p_copy(0, kv.at[my_slot], kv.at[my_slot], dev_h)
    to_h.start()
    wo_load = load(wo_hbm, wo)
    wc_loads = [
        load(wq_hbm, wc.at[:, 0:640]),
        load(wk_hbm, wc.at[:, 640:768]),
        load(wv_hbm, wc.at[:, 768:896]),
    ]
    dkv[...] = jnp.zeros_like(dkv)
    other_slot = core * 8 + z * 2 + 1 - xh
    p_copy(0, kv.at[other_slot], kv.at[other_slot], dev_h).wait_recv()
    to_z = []
    for k in range(3):
        pair = kv.at[pl.ds(core * 8 + z * 2, 2)]
        copy = p_copy(1 + k, pair, pair, dev_z[k])
        copy.start()
        to_z.append(copy)
    for copy in own_keys + own_q:
        copy.wait()
    for k in range(3):
        pair = kv.at[pl.ds(core * 8 + ((z + 3 - k) % 4) * 2, 2)]
        p_copy(1 + k, pair, pair, dev_z[k]).wait_recv()
    lane_half = kv.at[pl.ds(core * 8, 8)]
    to_s = p_copy(4, lane_half, lane_half, dev_s)
    to_s.start()
    other_half = kv.at[pl.ds((1 - core) * 8, 8)]
    p_copy(4, other_half, other_half, dev_s).wait_recv()

    def keys_of(c):
        return kv[pl.ds(c * 4, 4), :, 0:HEAD].reshape(CHUNK, HEAD)

    def values_of(c):
        return kv[pl.ds(c * 4, 4), :, HEAD : 2 * HEAD].reshape(CHUNK, HEAD)

    def flip(c, _):
        kt[c] = keys_of(c).astype(F32).T.astype(BF)
        vt[c] = values_of(c).astype(F32).T.astype(BF)
        return 0

    lax.fori_loop(0, 6, flip, 0)

    scaling = 1.0 / math.sqrt(HEAD)
    to_log2 = scaling * math.log2(math.e)

    def softmax(g):
        count = 5 + g

        def first(c, tops):
            keys = keys_of(c)
            gap = lax.broadcasted_iota(jnp.int32, (CHUNK, GROUP), 0) - lax.broadcasted_iota(
                jnp.int32, (CHUNK, GROUP), 1
            )
            seen = gap <= (g + 4 - c) * CHUNK
            new = []
            for h in range(HEADS):
                s = dot_nt(keys, q[g, h]) * to_log2
                s = jnp.where(seen, s, -1e30)
                scores[c, :, h * GROUP : (h + 1) * GROUP] = s
                new.append(jnp.maximum(tops[h], jnp.max(s, axis=0, keepdims=True)))
            return tuple(new)

        tops = lax.fori_loop(
            0, count, first, tuple(jnp.full((1, GROUP), -1e30, F32) for _ in range(HEADS))
        )

        def second(c, sums):
            new = []
            for h in range(HEADS):
                lanes = slice(h * GROUP, (h + 1) * GROUP)
                e = jnp.exp2(scores[c, :, lanes] - tops[h])
                scores[c, :, lanes] = e
                new.append(sums[h] + jnp.sum(e, axis=0, keepdims=True))
            return tuple(new)

        sums = lax.fori_loop(
            0, count, second, tuple(jnp.zeros((1, GROUP), F32) for _ in range(HEADS))
        )
        inverse = [1.0 / s for s in sums]
        out_t[g] = jnp.zeros((HEAD, LANES), F32)

        def third(c, _):
            for h in range(HEADS):
                lanes = slice(h * GROUP, (h + 1) * GROUP)
                p = (scores[c, :, lanes] * inverse[h]).astype(BF)
                prob[g, c, :, lanes] = p
                out_t[g, :, lanes] += dot(vt[c], p)
            return 0

        lax.fori_loop(0, count, third, 0)

    def attend(g):
        go_acc[...] = jnp.zeros_like(go_acc)

        def project(k, _):
            cols = pl.ds(pl.multiple_of(k * QUARTER, QUARTER), QUARTER)
            rows = blocks[pl.ds(g * 4, 4), :, cols].reshape(GROUP, QUARTER)
            go_acc[...] += dot_nt(rows, wo[:, cols])
            return 0

        lax.fori_loop(0, 4, project, 0)
        for h in range(HEADS):
            lanes = slice(h * GROUP, (h + 1) * GROUP)
            part = go_acc[:, h * HEAD : (h + 1) * HEAD].astype(BF)
            go[g, h] = part
            delta[0:1, lanes] = jnp.sum(
                part.astype(F32).T * out_t[g, :, lanes], axis=0, keepdims=True
            )
        dq_t[...] = jnp.zeros_like(dq_t)

        def step(c, _):
            values = values_of(c)
            for h in range(HEADS):
                lanes = slice(h * GROUP, (h + 1) * GROUP)
                dp = dot_nt(values, go[g, h])
                p = prob[g, c, :, lanes].astype(F32)
                ds[:, lanes] = (p * (dp - delta[0:1, lanes])).astype(BF)
            dk = dot(ds[...], q[g].reshape(LANES, HEAD))
            dv = dot(prob[g, c], go[g].reshape(LANES, HEAD))
            dkv[pl.ds(c * 4, 4), :, 0:HEAD] += dk.reshape(4, ROWS, HEAD)
            dkv[pl.ds(c * 4, 4), :, HEAD : 2 * HEAD] += dv.reshape(4, ROWS, HEAD)
            dq_t[...] += dot(kt[c], ds[...])
            return 0

        lax.fori_loop(0, 5 + g, step, 0)
        for h in range(HEADS):
            dq = (dq_t[:, h * GROUP : (h + 1) * GROUP] * scaling).T.astype(BF)
            grads[pl.ds(pl.multiple_of(g * GROUP, GROUP), GROUP), h * HEAD : (h + 1) * HEAD] = dq

    softmax(xl)

    g_wait(0, i_x, whole)
    g_wait(1, i_d, whole)
    g_wait(2, i_u, whole)
    send(3, i_d, h0, dev_u)
    send(4, i_u, h1, dev_d)
    send(5, i_u, h0, dev_x)
    send(6, i_d, h0, dev_x)
    send(7, i_x, h1, dev_u)
    send(8, i_x, h1, dev_d)

    softmax(ox)
    wo_load.wait()

    g_wait(3, i_f, h0)
    g_wait(4, i_f, h1)
    send(9, i_f, h0, dev_x)

    attend(xl)

    g_wait(5, i_xu, h0)
    g_wait(6, i_xd, h0)
    g_wait(7, i_xd, h1)
    g_wait(8, i_xu, h1)
    send(10, i_xd, q3, dev_u)
    send(11, i_xu, q2, dev_d)
    g_wait(9, i_xf, h0)
    g_wait(10, i_xf, q3)
    g_wait(11, i_xf, q2)
    for copy in sent:
        copy.wait_send()

    attend(ox)
    to_h.wait_send()
    for copy in to_z:
        copy.wait_send()
    to_s.wait_send()
    grads[:, 640:768] = (
        (dkv[16:24, :, 0:HEAD] * scaling).astype(BF).reshape(8 * ROWS, HEAD)
    )
    grads[:, 768:896] = dkv[16:24, :, HEAD : 2 * HEAD].astype(BF).reshape(8 * ROWS, HEAD)

    dkv_scale = jnp.where(
        lax.broadcasted_iota(jnp.int32, (1, 1, 2 * HEAD), 2) < HEAD, scaling, 1.0
    ).astype(F32)
    p_send[...] = (dkv[pl.ds((1 - core) * 8, 8)] * dkv_scale).astype(BF)
    ps = p_copy(5, p_send, p_land, dev_s)
    ps.start()

    for copy in wc_loads:
        copy.wait()
    r_sent = []

    def r_copy(k, src, dst, dev):
        return pltpu.make_async_remote_copy(
            src_ref=src, dst_ref=dst, send_sem=rs_sem.at[k], recv_sem=rr_sem.at[k],
            device_id=dev, device_id_type=MESH,
        )

    low, high = pl.ds(0, HALF), pl.ds(HALF, HALF)
    c2, c3 = pl.ds(2 * QUARTER, QUARTER), pl.ds(3 * QUARTER, QUARTER)
    part = pl.ds(0, QUARTER)

    def r_send(k, slot, cols, dev, narrow=False):
        dst = landed.at[k, :, part] if narrow else landed.at[k]
        copy = r_copy(k, blocks.at[slot, :, cols], dst, dev)
        copy.start()
        r_sent.append(copy)

    def r_wait(k, narrow=False):
        dst = landed.at[k, :, part] if narrow else landed.at[k]
        r_copy(k, dst, dst, dev_x).wait_recv()

    def r_add(k, slot, cols, narrow=False):
        r_wait(k, narrow)
        got = landed[k, :, part] if narrow else landed[k]
        mine = blocks[slot, :, cols]
        blocks[slot, :, cols] = (mine.astype(F32) + got.astype(F32)).astype(BF)

    def term(g, n):
        rows = pl.ds(pl.multiple_of(g * GROUP, GROUP), GROUP)
        for k in range(5):
            start = n * QUARTER + k * 256
            value = dot_nt(grads[rows, :], wc[start : start + 256, :]).astype(BF)
            blocks[pl.ds(g * 4, 4), :, start : start + 256] = value.reshape(4, ROWS, 256)

    term(ox, 0)
    term(ox, 1)
    r_send(0, i_xf, low, dev_x)
    r_send(3, i_xu, low, dev_x)
    r_send(4, i_xd, low, dev_x)
    term(ox, 2)
    r_send(1, i_xf, c2, dev_u, True)
    term(ox, 3)
    r_send(2, i_xf, c3, dev_d, True)
    term(xl, 2)
    term(xl, 3)
    r_send(5, i_f, high, dev_u)
    r_send(9, i_d, high, dev_d)
    r_add(1, i_xu, c2, True)
    r_add(2, i_xd, c3, True)
    r_send(6, i_xu, high, dev_u)
    r_send(7, i_xd, high, dev_d)
    term(xl, 0)
    term(xl, 1)
    r_add(0, i_f, low)
    r_send(8, i_f, low, dev_d)
    r_send(10, i_x, low, dev_x)

    def p_recv(k, dst, dev):
        p_copy(k, dst, dst, dev).wait_recv()

    ps.wait_send()
    p_recv(5, p_land, dev_s)
    mine = dkv.at[pl.ds(core * 8, 8)]
    mine[...] = mine[...] * dkv_scale + p_land[...].astype(F32)
    p_send[...] = mine[...].astype(BF)
    z_copies = []
    for k in range(3):
        peer_z = (z + 1 + k) % 4
        copy = p_copy(6 + k, p_send.at[pl.ds(peer_z * 2, 2)], p_land_z.at[k], dev_z[k])
        copy.start()
        z_copies.append(copy)

    r_add(6, i_x, high)
    r_add(7, i_x, high)
    r_send(11, i_x, high, dev_x)
    r_add(5, i_u, high)
    r_send(12, i_u, high, dev_u)
    r_add(3, i_u, low)
    r_send(13, i_u, low, dev_u)
    r_add(4, i_d, low)
    r_add(8, i_d, low)
    last = r_copy(14, blocks.at[i_d, :, low], landed.at[14], dev_d)
    last.start()
    r_sent.append(last)

    for k in range(3):
        z_copies[k].wait_send()
        p_recv(6 + k, p_land_z.at[k], dev_z[k])
    pair_at = core * 8 + z * 2
    both = dkv[pl.ds(pair_at, 2)]
    for k in range(3):
        both = both + p_land_z[k].astype(F32)
    dkv[pl.ds(pair_at, 2)] = both
    p_send[0] = dkv[pair_at + 1 - xh].astype(BF)
    ph = p_copy(9, p_send.at[0], p_land_h, dev_h)
    ph.start()
    p_recv(9, p_land_h, dev_h)
    total = dkv[pair_at + xh] + p_land_h[...].astype(F32)
    pkg_ref[...] = total[:, 0:HEAD]
    pvg_ref[...] = total[:, HEAD : 2 * HEAD]
    ph.wait_send()

    for k in (9, 10, 11, 12, 13, 14):
        r_wait(k)
    out_ref[0, :, 0:HALF] = (
        (blocks[t, :, low].astype(F32) + landed[10].astype(F32))
        + (landed[13].astype(F32) + landed[14].astype(F32))
    ).astype(BF)
    out_ref[0, :, HALF:WIDTH] = (
        (blocks[t, :, high].astype(F32) + landed[11].astype(F32))
        + (landed[12].astype(F32) + landed[9].astype(F32))
    ).astype(BF)
    for copy in r_sent:
        copy.wait_send()


def body(
    queries,
    response_keys,
    response_values,
    prompt_key_rows,
    prompt_value_rows,
    upstream,
    lengths,
    query_weight,
    key_matrix,
    value_matrix,
    out_weight,
):
    vmem = pl.BlockSpec(memory_space=pltpu.VMEM)
    smem = pl.BlockSpec(memory_space=pltpu.SMEM)
    hbm = pl.BlockSpec(memory_space=pl.ANY)
    dma = pltpu.SemaphoreType.DMA
    return pl.pallas_call(
        kernel,
        out_shape=(
            jax.ShapeDtypeStruct((1, ROWS, WIDTH), BF),
            jax.ShapeDtypeStruct((ROWS, HEAD), F32),
            jax.ShapeDtypeStruct((ROWS, HEAD), F32),
        ),
        in_specs=[smem, hbm, hbm, hbm, hbm, hbm, vmem, hbm, hbm, hbm, hbm],
        out_specs=(vmem, vmem, vmem),
        scratch_shapes=[
            pltpu.VMEM((8, ROWS, WIDTH), BF),
            pltpu.VMEM((HEADS * HEAD, WIDTH), BF),
            pltpu.VMEM((WIDTH, 896), BF),
            pltpu.VMEM((2, HEADS, GROUP, HEAD), BF),
            pltpu.VMEM((24, ROWS, 2 * HEAD), BF),
            pltpu.VMEM((6, HEAD, CHUNK), BF),
            pltpu.VMEM((6, HEAD, CHUNK), BF),
            pltpu.VMEM((6, CHUNK, LANES), F32),
            pltpu.VMEM((2, 6, CHUNK, LANES), BF),
            pltpu.VMEM((2, HEAD, LANES), F32),
            pltpu.VMEM((GROUP, HEADS * HEAD), F32),
            pltpu.VMEM((2, HEADS, GROUP, HEAD), BF),
            pltpu.VMEM((8, LANES), F32),
            pltpu.VMEM((CHUNK, LANES), BF),
            pltpu.VMEM((HEAD, LANES), F32),
            pltpu.VMEM((24, ROWS, 2 * HEAD), F32),
            pltpu.VMEM((8 * ROWS, 896), BF),
            pltpu.VMEM((15, ROWS, HALF), BF),
            pltpu.VMEM((8, ROWS, 2 * HEAD), BF),
            pltpu.VMEM((8, ROWS, 2 * HEAD), BF),
            pltpu.VMEM((3, 2, ROWS, 2 * HEAD), BF),
            pltpu.VMEM((ROWS, 2 * HEAD), BF),
            dma((32,)),
            dma((12,)),
            dma((12,)),
            dma((15,)),
            dma((15,)),
            dma((10,)),
            dma((10,)),
        ],
        compiler_params=pltpu.CompilerParams(
            collective_id=0, has_side_effects=True, vmem_limit_bytes=62 * 1024 * 1024
        ),
        cost_estimate=pl.CostEstimate(
            flops=18_000_000_000, bytes_accessed=20_000_000, transcendentals=4_000_000
        ),
    )(
        lengths,
        queries,
        response_keys,
        response_values,
        prompt_key_rows,
        prompt_value_rows,
        upstream,
        query_weight,
        key_matrix,
        value_matrix,
        out_weight,
    )


def solution(mesh):
    in_specs = (
        P("resp", None, "tp"),
        P("resp", None, "tp"),
        P("resp", None, "tp"),
        P("resp", "tp"),
        P("resp", "tp"),
        P("resp", "tp", None),
        P("resp"),
        P(None, "tp"),
        P(None, "tp"),
        P(None, "tp"),
        P("tp", None),
    )
    out_specs = (P("resp", "tp", None), P("resp", "tp"), P("resp", "tp"))
    return jax.shard_map(body, mesh=mesh, in_specs=in_specs, out_specs=out_specs, check_vma=False)
```

```python
import functools
import math

import jax
import jax.numpy as jnp
from jax import lax
from jax.experimental import pallas as pl
from jax.experimental.pallas import tpu as pltpu
from jax.sharding import PartitionSpec as P

MESH = pl.DeviceIdType.MESH
BF = jnp.bfloat16
F32 = jnp.float32
WIDTH = 5120
HEADS = 5
HEAD = 128
ROWS = 64
SUB = 128
CHUNK = 256
LANES = HEADS * SUB
QUARTER = WIDTH // 4
PIECE = 16

ORDER = ("o", "U", "D", "X", "F", "XU", "XD", "XF")
POS = {name: i for i, name in enumerate(ORDER)}
RENAME = {
    "X": {"o": "X", "D": "XD", "U": "XU", "F": "XF", "X": "o", "XU": "U", "XD": "D", "XF": "F"},
    "U": {"o": "D", "D": "F", "X": "XD", "XD": "XF", "F": "U", "XF": "XU", "U": "o", "XU": "X"},
    "D": {"o": "U", "U": "F", "X": "XU", "XU": "XF", "F": "D", "XF": "XD", "D": "o", "XD": "X"},
}
W = WIDTH
GATHER = {
    "X": (("o", 3, 0, W), ("o", 2, 0, W), ("o", 1, 0, W), ("o", 0, 0, W), ("D", 0, 0, W), ("D", 1, 0, W),
          ("U", 0, 0, W), ("U", 1, 0, W), ("F", 0, 0, W), ("F", 1, 0, 1792)),
    "U": (("o", 0, 0, W), ("o", 1, 0, W), ("o", 2, 0, W), ("o", 3, 0, W), ("X", 3, 0, W), ("D", 0, 0, W),
          ("D", 1, 0, W), ("X", 2, 0, W), ("XD", 3, 0, W), ("XD", 1, 1792, 1664)),
    "D": (("o", 2, 0, W), ("o", 3, 0, W), ("o", 0, 0, W), ("o", 1, 0, W), ("X", 2, 0, W), ("U", 2, 0, W),
          ("U", 3, 0, W), ("X", 3, 0, W), ("XU", 2, 0, W), ("XU", 1, 3456, 1664)),
}
Q = QUARTER
REDUCE = {
    "X": (("XF", 1, 0, 512), ("XF", 0, 0, Q), ("XU", 1, 0, Q), ("XU", 0, 0, Q), ("XD", 1, 0, Q), ("XD", 0, 0, Q),
          ("X", 0, 0, Q), ("X", 1, 0, Q), ("X", 2, 0, Q), ("X", 3, 0, Q)),
    "U": (("XF", 1, 896, 384), ("XF", 2, 0, Q), ("XU", 3, 0, Q), ("F", 3, 0, Q), ("F", 2, 0, Q), ("XU", 2, 0, Q),
          ("U", 1, 0, Q), ("U", 0, 0, Q), ("U", 3, 0, Q), ("U", 2, 0, Q)),
    "D": (("XF", 1, 512, 384), ("XF", 3, 0, Q), ("XD", 2, 0, Q), ("D", 3, 0, Q), ("D", 2, 0, Q), ("F", 1, 0, Q),
          ("F", 0, 0, Q), ("XD", 3, 0, Q), ("D", 1, 0, Q), ("D", 0, 0, Q)),
}
LINKS = ("X", "U", "D")


def number(plan):
    keys = [(link, i) for link in LINKS for i in range(len(plan[link]))]
    return {key: n for n, key in enumerate(keys)}


def arrivals(plan):
    found = {}
    numbers = number(plan)
    for i in range(10):
        for link in LINKS:
            block, quarter, at, size = plan[link][i]
            key = (RENAME[link][block], quarter)
            found.setdefault(key, []).append((numbers[link, i], at, size))
    return found
NT = (((1,), (1,)), ((), ()))


def dot_nt(a, b):
    return lax.dot_general(a, b, NT, preferred_element_type=F32)


def dot(a, b):
    return jnp.dot(a, b, preferred_element_type=F32)


def kernel(
    len_ref,
    q_hbm,
    rk_hbm,
    rv_hbm,
    pk_hbm,
    pv_hbm,
    up_ref,
    wq_hbm,
    wk_hbm,
    wv_hbm,
    wo_hbm,
    out_ref,
    pg_ref,
    blocks,
    wo,
    wc,
    q,
    kv,
    kt,
    vt,
    scores,
    prob,
    out_t,
    go_acc,
    go,
    delta,
    ds,
    dq_t,
    dkv,
    grads,
    landed,
    p_send,
    p_land,
    p_land_z,
    p_land_h,
    load_sem,
    gs_sem,
    gr_sem,
    rs_sem,
    rr_sem,
    ps_sem,
    pr_sem,
):
    r = lax.axis_index("resp")
    t = lax.axis_index("tp")
    z, xh, core = r // 4, (r // 2) % 2, r % 2
    xl, y = t // 4, t % 4
    up1, down1, far1 = (y + 1) % 4, (y + 3) % 4, (y + 2) % 4
    own, other = xl * 4, (1 - xl) * 4
    ids = [t, own + up1, own + down1, other + y, own + far1, other + up1, other + down1, other + far1]
    device = {"X": (r, ids[3]), "U": (r, ids[1]), "D": (r, ids[2])}
    dev_s = (z * 4 + xh * 2 + 1 - core, t)
    dev_h = (z * 4 + (1 - xh) * 2 + core, t)
    dev_z = [(((z + k) % 4) * 4 + xh * 2 + core, t) for k in (1, 2, 3)]

    barrier = pltpu.get_barrier_semaphore()
    peers = list(device.values()) + [dev_s, dev_h] + dev_z
    for peer in peers:
        pl.semaphore_signal(barrier, inc=1, device_id=peer, device_id_type=MESH)

    loads = []

    def load(src, dst):
        copy = pltpu.make_async_copy(src, dst, load_sem.at[len(loads)])
        copy.start()
        loads.append(copy)
        return copy

    my_slot = core * 8 + z * 2 + xh
    own_prompt = [
        load(pk_hbm, kv.at[my_slot, :, 0:HEAD]),
        load(pv_hbm, kv.at[my_slot, :, HEAD : 2 * HEAD]),
    ]
    own_q = [
        load(
            q_hbm.at[0, pl.ds(pl.multiple_of(ids[p] * ROWS, ROWS), ROWS)],
            grads.at[pl.ds(p * ROWS, ROWS), 0:640],
        )
        for p in range(8)
    ]
    own_keys = []
    for i in range(8):
        rows = pl.ds(i * ROWS, ROWS)
        own_keys.append(load(rk_hbm.at[0, rows], kv.at[16 + i, :, 0:HEAD]))
        own_keys.append(load(rv_hbm.at[0, rows], kv.at[16 + i, :, HEAD : 2 * HEAD]))

    position = t * ROWS + lax.broadcasted_iota(jnp.int32, (ROWS, WIDTH), 0)
    live = position < len_ref[0]
    blocks[0] = jnp.where(live, up_ref[0], jnp.zeros((), BF))

    pl.semaphore_wait(barrier, len(peers))

    def p_copy(k, src, dst, dev):
        return pltpu.make_async_remote_copy(
            src_ref=src, dst_ref=dst, send_sem=ps_sem.at[k], recv_sem=pr_sem.at[k],
            device_id=dev, device_id_type=MESH,
        )

    def p_recv(k, dst, dev):
        p_copy(k, dst, dst, dev).wait_recv()

    for copy in own_prompt:
        copy.wait()
    to_h = p_copy(0, kv.at[my_slot], kv.at[my_slot], dev_h)
    to_h.start()

    g_number, g_arrive = number(GATHER), arrivals(GATHER)
    g_sent, g_seen, g_next = [], set(), {link: 0 for link in LINKS}

    def g_copy(k, src_name, dst_name, quarter, at, size, dev):
        rows, cols = pl.ds(quarter * PIECE, PIECE), pl.ds(at, size)
        return pltpu.make_async_remote_copy(
            src_ref=blocks.at[POS[src_name], rows, cols],
            dst_ref=blocks.at[POS[dst_name], rows, cols],
            send_sem=gs_sem.at[k], recv_sem=gr_sem.at[k], device_id=dev, device_id_type=MESH,
        )

    def g_have(name, quarters=(0, 1, 2, 3)):
        for quarter in quarters:
            if name == "o" or (name, quarter) in g_seen:
                continue
            g_seen.add((name, quarter))
            for k, at, size in g_arrive[name, quarter]:
                g_copy(k, name, name, quarter, at, size, device["X"]).wait_recv()

    def g_send(link, count):
        for _ in range(count):
            i = g_next[link]
            g_next[link] = i + 1
            name, quarter, at, size = GATHER[link][i]
            g_have(name, (quarter,))
            copy = g_copy(
                g_number[link, i], name, RENAME[link][name], quarter, at, size, device[link]
            )
            copy.start()
            g_sent.append(copy)

    for _ in range(4):
        for link in LINKS:
            g_send(link, 1)

    wo_load = load(wo_hbm, wo)
    wc_loads = [
        load(wq_hbm, wc.at[:, 0:640]),
        load(wk_hbm, wc.at[:, 640:768]),
        load(wv_hbm, wc.at[:, 768:896]),
    ]
    p_recv(0, kv.at[core * 8 + z * 2 + 1 - xh], dev_h)
    to_z = []
    for k in range(3):
        pair = kv.at[pl.ds(core * 8 + z * 2, 2)]
        copy = p_copy(1 + k, pair, pair, dev_z[k])
        copy.start()
        to_z.append(copy)
    dkv[...] = jnp.zeros_like(dkv)
    for copy in own_q:
        copy.wait()
    for s in range(4):
        for h in range(HEADS):
            q[s, h] = grads[s * SUB : (s + 1) * SUB, h * HEAD : (h + 1) * HEAD]
    for copy in own_keys:
        copy.wait()

    def keys_of(c):
        return kv[pl.ds(c * 4, 4), :, 0:HEAD].reshape(CHUNK, HEAD)

    def values_of(c):
        return kv[pl.ds(c * 4, 4), :, HEAD : 2 * HEAD].reshape(CHUNK, HEAD)

    def flip(c, _):
        kt[c] = keys_of(c).astype(F32).T.astype(BF)
        vt[c] = values_of(c).astype(F32).T.astype(BF)
        return 0

    lax.fori_loop(4, 6, flip, 0)
    for k in range(3):
        p_recv(1 + k, kv.at[pl.ds(core * 8 + ((z + 3 - k) % 4) * 2, 2)], dev_z[k])
    lane_half = kv.at[pl.ds(core * 8, 8)]
    to_s = p_copy(4, lane_half, lane_half, dev_s)
    to_s.start()
    p_recv(4, kv.at[pl.ds((1 - core) * 8, 8)], dev_s)
    lax.fori_loop(0, 4, flip, 0)

    scaling = 1.0 / math.sqrt(HEAD)
    to_log2 = scaling * math.log2(math.e)

    def softmax(s):
        lane = lax.broadcasted_iota(jnp.int32, (1, SUB), 1)
        row = jnp.where(lane < ROWS, ids[2 * s] * ROWS, ids[2 * s + 1] * ROWS - ROWS) + lane
        q_rows = q[s].reshape(LANES, HEAD)

        def first(c, tops):
            key_at = (c - 4) * CHUNK + lax.broadcasted_iota(jnp.int32, (CHUNK, SUB), 0)
            seen = key_at <= row
            all_heads = dot_nt(keys_of(c), q_rows)
            new = []
            for h in range(HEADS):
                lanes = slice(h * SUB, (h + 1) * SUB)
                part = jnp.where(seen, all_heads[:, lanes] * to_log2, -1e30)
                scores[c, :, lanes] = part
                new.append(jnp.maximum(tops[h], jnp.max(part, axis=0, keepdims=True)))
            return tuple(new)

        tops = lax.fori_loop(
            0, 6, first, tuple(jnp.full((1, SUB), -1e30, F32) for _ in range(HEADS))
        )

        def second(c, sums):
            new = []
            for h in range(HEADS):
                lanes = slice(h * SUB, (h + 1) * SUB)
                e = jnp.exp2(scores[c, :, lanes] - tops[h])
                scores[c, :, lanes] = e
                new.append(sums[h] + jnp.sum(e, axis=0, keepdims=True))
            return tuple(new)

        sums = lax.fori_loop(
            0, 6, second, tuple(jnp.zeros((1, SUB), F32) for _ in range(HEADS))
        )
        inverse = [1.0 / total for total in sums]
        out_t[s] = jnp.zeros((HEAD, LANES), F32)

        def third(c, _):
            for h in range(HEADS):
                lanes = slice(h * SUB, (h + 1) * SUB)
                prob[s, c, :, lanes] = (scores[c, :, lanes] * inverse[h]).astype(BF)
            out_t[s] += dot(vt[c], prob[s, c])
            return 0

        lax.fori_loop(0, 6, third, 0)

    def attend(subs):
        first, count = subs[0], len(subs)
        rows = count * SUB
        go_acc[0:rows] = jnp.zeros((rows, HEADS * HEAD), F32)

        def project(k, _):
            cols = pl.ds(pl.multiple_of(k * QUARTER, QUARTER), QUARTER)
            part = blocks[2 * first : 2 * (first + count), :, cols].reshape(rows, QUARTER)
            go_acc[0:rows] += dot_nt(part, wo[:, cols])
            return 0

        lax.fori_loop(0, 4, project, 0)
        for j, s in enumerate(subs):
            for h in range(HEADS):
                lanes = slice(h * SUB, (h + 1) * SUB)
                part = go_acc[j * SUB : (j + 1) * SUB, h * HEAD : (h + 1) * HEAD].astype(BF)
                go[s, h] = part
                delta[s, 0:1, lanes] = jnp.sum(
                    part.astype(F32).T * out_t[s, :, lanes], axis=0, keepdims=True
                )
        wide = count * LANES
        dq_t[:, 0:wide] = jnp.zeros((HEAD, wide), F32)

        def step(c, _):
            values = values_of(c)
            dv = jnp.zeros((CHUNK, HEAD), F32)
            for j, s in enumerate(subs):
                dp = dot_nt(values, go[s].reshape(LANES, HEAD))
                for h in range(HEADS):
                    lanes = slice(h * SUB, (h + 1) * SUB)
                    p = prob[s, c, :, lanes].astype(F32)
                    ds[:, j * LANES + h * SUB : j * LANES + (h + 1) * SUB] = (
                        p * (dp[:, lanes] - delta[s, 0:1, lanes])
                    ).astype(BF)
                dv = dv + dot(prob[s, c], go[s].reshape(LANES, HEAD))
            dk = dot(ds[:, 0:wide], q[first : first + count].reshape(wide, HEAD))
            dkv[pl.ds(c * 4, 4), :, 0:HEAD] += dk.reshape(4, ROWS, HEAD)
            dkv[pl.ds(c * 4, 4), :, HEAD : 2 * HEAD] += dv.reshape(4, ROWS, HEAD)
            dq_t[:, 0:wide] += dot(kt[c], ds[:, 0:wide])
            return 0

        lax.fori_loop(0, 6, step, 0)
        for j, s in enumerate(subs):
            for h in range(HEADS):
                at = j * LANES + h * SUB
                grads[s * SUB : (s + 1) * SUB, h * HEAD : (h + 1) * HEAD] = (
                    (dq_t[:, at : at + SUB] * scaling).T.astype(BF)
                )

    for link in ("U", "D"):
        g_send(link, 4)
    g_send("X", 2)
    softmax(0)
    softmax(1)
    wo_load.wait()
    g_send("X", 2)
    for name in ("U", "D", "X"):
        g_have(name)
    attend((0, 1))
    softmax(2)
    for link in ("X", "U", "D"):
        g_send(link, 2)
    softmax(3)
    g_have("F")
    g_have("XU")
    attend((2,))
    g_have("XD")
    g_have("XF")
    for copy in g_sent:
        copy.wait_send()
    attend((3,))
    to_h.wait_send()
    for copy in to_z:
        copy.wait_send()
    to_s.wait_send()

    dkv_scale = jnp.where(
        lax.broadcasted_iota(jnp.int32, (1, 1, 2 * HEAD), 2) < HEAD, scaling, 1.0
    ).astype(F32)
    for p in range(8):
        grads[p * ROWS : (p + 1) * ROWS, 640:896] = (dkv[16 + ids[p]] * dkv_scale[0]).astype(BF)
    for copy in wc_loads:
        copy.wait()

    r_number, r_arrive = number(REDUCE), arrivals(REDUCE)
    r_sent, r_seen, r_next = [], set(), {link: 0 for link in LINKS}

    def r_copy(k, src, size, dev):
        return pltpu.make_async_remote_copy(
            src_ref=src, dst_ref=landed.at[k, :, pl.ds(0, size)],
            send_sem=rs_sem.at[k], recv_sem=rr_sem.at[k], device_id=dev, device_id_type=MESH,
        )

    def r_wait(k, size):
        r_copy(k, landed.at[k, :, pl.ds(0, size)], size, device["X"]).wait_recv()

    def r_add(name, quarter):
        if (name, quarter) in r_seen:
            return
        r_seen.add((name, quarter))
        for k, at, size in r_arrive.get((name, quarter), ()):
            r_wait(k, size)
            cols = pl.ds(quarter * QUARTER + at, size)
            mine = blocks[POS[name], :, cols].astype(F32)
            blocks[POS[name], :, cols] = (mine + landed[k, :, 0:size].astype(F32)).astype(BF)

    def r_send(link, count):
        for _ in range(count):
            i = r_next[link]
            r_next[link] = i + 1
            name, quarter, at, size = REDUCE[link][i]
            r_add(name, quarter)
            k = r_number[link, i]
            src = blocks.at[POS[name], :, pl.ds(quarter * QUARTER + at, size)]
            copy = r_copy(k, src, size, device[link])
            copy.start()
            r_sent.append(copy)

    def term(half, quarter):
        rows = slice(half * 256, half * 256 + 256)
        for k in range(5):
            start = quarter * QUARTER + k * 256
            value = dot_nt(grads[rows, :], wc[start : start + 256, :]).astype(BF)
            blocks[half * 4 : half * 4 + 4, :, start : start + 256] = value.reshape(4, ROWS, 256)

    term(1, 1)
    for link in LINKS:
        r_send(link, 1)
    term(1, 2)
    r_send("U", 1)
    term(1, 3)
    r_send("D", 1)
    r_send("U", 2)
    term(1, 0)
    r_send("X", 5)
    r_send("U", 1)
    r_send("D", 1)
    p_send[...] = (dkv[pl.ds((1 - core) * 8, 8)] * dkv_scale).astype(BF)
    ps = p_copy(5, p_send, p_land, dev_s)
    ps.start()
    term(0, 3)
    r_send("D", 1)
    term(0, 2)
    r_send("D", 1)
    term(0, 0)
    term(0, 1)
    r_send("D", 3)
    r_send("U", 1)
    r_send("X", 2)

    ps.wait_send()
    p_recv(5, p_land, dev_s)
    mine = pl.ds(core * 8, 8)
    dkv[mine] = dkv[mine] * dkv_scale + p_land[...].astype(F32)
    p_send[...] = dkv[mine].astype(BF)
    z_copies = []
    for k in range(3):
        peer_z = (z + 1 + k) % 4
        copy = p_copy(6 + k, p_send.at[pl.ds(peer_z * 2, 2)], p_land_z.at[k], dev_z[k])
        copy.start()
        z_copies.append(copy)

    r_send("U", 4)

    for k in range(3):
        z_copies[k].wait_send()
        p_recv(6 + k, p_land_z.at[k], dev_z[k])
    pair_at = core * 8 + z * 2
    both = dkv[pl.ds(pair_at, 2)]
    for k in range(3):
        both = both + p_land_z[k].astype(F32)
    dkv[pl.ds(pair_at, 2)] = both
    p_send[0] = dkv[pair_at + 1 - xh].astype(BF)
    ph = p_copy(9, p_send.at[0], p_land_h, dev_h)
    ph.start()

    r_send("D", 2)
    r_send("X", 1)
    p_recv(9, p_land_h, dev_h)
    pg_ref[...] = dkv[pair_at + xh] + p_land_h[...].astype(F32)
    r_send("X", 1)
    ph.wait_send()

    for quarter in (0, 1, 2, 3):
        cols = slice(quarter * QUARTER, (quarter + 1) * QUARTER)
        total = blocks[0, :, cols].astype(F32)
        for k, at, size in r_arrive["o", quarter]:
            r_wait(k, size)
            total = total + landed[k].astype(F32)
        out_ref[0, :, cols] = total.astype(BF)
    for copy in r_sent:
        copy.wait_send()


def split_kernel(rows_ref, both_ref, out_ref, key_ref, value_ref):
    out_ref[...] = rows_ref[...]
    key_ref[...] = both_ref[:, 0:HEAD]
    value_ref[...] = both_ref[:, HEAD : 2 * HEAD]


def split(input_grad, prompt_grads):
    vmem = pl.BlockSpec(memory_space=pltpu.VMEM)
    return pl.pallas_call(
        split_kernel,
        out_shape=(
            jax.ShapeDtypeStruct((1, ROWS, WIDTH), BF),
            jax.ShapeDtypeStruct((ROWS, HEAD), F32),
            jax.ShapeDtypeStruct((ROWS, HEAD), F32),
        ),
        in_specs=[vmem, vmem],
        out_specs=(vmem, vmem, vmem),
    )(input_grad, prompt_grads)


def body(
    queries,
    response_keys,
    response_values,
    prompt_key_rows,
    prompt_value_rows,
    upstream,
    lengths,
    query_weight,
    key_matrix,
    value_matrix,
    out_weight,
):
    vmem = pl.BlockSpec(memory_space=pltpu.VMEM)
    smem = pl.BlockSpec(memory_space=pltpu.SMEM)
    hbm = pl.BlockSpec(memory_space=pl.ANY)
    dma = pltpu.SemaphoreType.DMA
    input_grad, prompt_grads = pl.pallas_call(
        kernel,
        out_shape=(
            jax.ShapeDtypeStruct((1, ROWS, WIDTH), BF),
            jax.ShapeDtypeStruct((ROWS, 2 * HEAD), F32),
        ),
        in_specs=[smem, hbm, hbm, hbm, hbm, hbm, vmem, hbm, hbm, hbm, hbm],
        out_specs=(vmem, vmem),
        scratch_shapes=[
            pltpu.VMEM((8, ROWS, WIDTH), BF),
            pltpu.VMEM((HEADS * HEAD, WIDTH), BF),
            pltpu.VMEM((WIDTH, 896), BF),
            pltpu.VMEM((4, HEADS, SUB, HEAD), BF),
            pltpu.VMEM((24, ROWS, 2 * HEAD), BF),
            pltpu.VMEM((6, HEAD, CHUNK), BF),
            pltpu.VMEM((6, HEAD, CHUNK), BF),
            pltpu.VMEM((6, CHUNK, LANES), F32),
            pltpu.VMEM((4, 6, CHUNK, LANES), BF),
            pltpu.VMEM((4, HEAD, LANES), F32),
            pltpu.VMEM((2 * SUB, HEADS * HEAD), F32),
            pltpu.VMEM((4, HEADS, SUB, HEAD), BF),
            pltpu.VMEM((4, 8, LANES), F32),
            pltpu.VMEM((CHUNK, 2 * LANES), BF),
            pltpu.VMEM((HEAD, 2 * LANES), F32),
            pltpu.VMEM((24, ROWS, 2 * HEAD), F32),
            pltpu.VMEM((8 * ROWS, 896), BF),
            pltpu.VMEM((30, ROWS, QUARTER), BF),
            pltpu.VMEM((8, ROWS, 2 * HEAD), BF),
            pltpu.VMEM((8, ROWS, 2 * HEAD), BF),
            pltpu.VMEM((3, 2, ROWS, 2 * HEAD), BF),
            pltpu.VMEM((ROWS, 2 * HEAD), BF),
            dma((32,)),
            dma((30,)),
            dma((30,)),
            dma((30,)),
            dma((30,)),
            dma((10,)),
            dma((10,)),
        ],
        compiler_params=pltpu.CompilerParams(
            collective_id=0, has_side_effects=True, vmem_limit_bytes=62 * 1024 * 1024
        ),
        cost_estimate=pl.CostEstimate(
            flops=18_000_000_000, bytes_accessed=20_000_000, transcendentals=4_000_000
        ),
    )(
        lengths,
        queries,
        response_keys,
        response_values,
        prompt_key_rows,
        prompt_value_rows,
        upstream,
        query_weight,
        key_matrix,
        value_matrix,
        out_weight,
    )
    return split(input_grad, prompt_grads)


def solution(mesh):
    in_specs = (
        P("resp", None, "tp"),
        P("resp", None, "tp"),
        P("resp", None, "tp"),
        P("resp", "tp"),
        P("resp", "tp"),
        P("resp", "tp", None),
        P("resp"),
        P(None, "tp"),
        P(None, "tp"),
        P(None, "tp"),
        P("tp", None),
    )
    out_specs = (P("resp", "tp", None), P("resp", "tp"), P("resp", "tp"))
    return jax.shard_map(body, mesh=mesh, in_specs=in_specs, out_specs=out_specs, check_vma=False)
```

```python
import functools
import math

import jax
import jax.numpy as jnp
from jax import lax
from jax.experimental import pallas as pl
from jax.experimental.pallas import tpu as pltpu
from jax.sharding import PartitionSpec as P

MESH = pl.DeviceIdType.MESH
BF = jnp.bfloat16
F32 = jnp.float32
WIDTH = 5120
HEADS = 5
HEAD = 128
ROWS = 64
SUB = 128
CHUNK = 256
LANES = HEADS * SUB
QUARTER = WIDTH // 4

ORDER = ("o", "U", "D", "X", "F", "XU", "XD", "XF")
POS = {name: i for i, name in enumerate(ORDER)}
RENAME = {
    "X": {"o": "X", "D": "XD", "U": "XU", "F": "XF", "X": "o", "XU": "U", "XD": "D", "XF": "F"},
    "U": {"o": "D", "D": "F", "X": "XD", "XD": "XF", "F": "U", "XF": "XU", "U": "o", "XU": "X"},
    "D": {"o": "U", "U": "F", "X": "XU", "XU": "XF", "F": "D", "XF": "XD", "D": "o", "XD": "X"},
}
Q = QUARTER
A = 896
B = Q - A
GATHER = {
    "X": (("o", 3, 0, Q), ("o", 2, 0, Q), ("o", 1, 0, Q), ("o", 0, 0, Q), ("D", 0, 0, A), ("D", 1, 0, Q),
          ("U", 0, 0, A), ("U", 1, 0, Q), ("F", 0, 0, Q), ("F", 1, 0, Q)),
    "U": (("o", 0, 0, Q), ("o", 1, 0, Q), ("o", 2, 0, Q), ("o", 3, 0, Q), ("X", 3, 0, Q), ("D", 0, 0, Q),
          ("D", 1, 0, Q), ("X", 0, A, B), ("X", 2, 0, Q), ("XD", 3, 0, Q)),
    "D": (("o", 2, 0, Q), ("o", 3, 0, Q), ("o", 0, 0, Q), ("o", 1, 0, Q), ("X", 2, 0, Q), ("U", 2, 0, Q),
          ("U", 3, 0, Q), ("X", 0, A, B), ("X", 3, 0, Q), ("XU", 2, 0, Q)),
}
REDUCE = {
    "X": (("XF", 1, 0, Q), ("XU", 1, 0, Q), ("XD", 1, 0, Q), ("XF", 0, 0, Q), ("XU", 0, 0, A), ("XD", 0, 0, A),
          ("X", 1, 0, Q), ("X", 2, 0, Q), ("X", 0, 0, Q), ("X", 3, 0, Q)),
    "U": (("XU", 3, 0, Q), ("F", 3, 0, Q), ("XF", 2, 0, Q), ("F", 2, 0, Q), ("XU", 0, A, B), ("XU", 2, 0, Q),
          ("U", 1, 0, Q), ("U", 0, 0, Q), ("U", 3, 0, Q), ("U", 2, 0, Q)),
    "D": (("XF", 3, 0, Q), ("XD", 2, 0, Q), ("D", 3, 0, Q), ("D", 2, 0, Q), ("XD", 0, A, B), ("F", 1, 0, Q),
          ("F", 0, 0, Q), ("XD", 3, 0, Q), ("D", 1, 0, Q), ("D", 0, 0, Q)),
}
LINKS = ("X", "U", "D")


def number(plan):
    keys = [(link, i) for link in LINKS for i in range(len(plan[link]))]
    return {key: n for n, key in enumerate(keys)}


def arrivals(plan):
    found = {}
    numbers = number(plan)
    for i in range(10):
        for link in LINKS:
            block, quarter, at, size = plan[link][i]
            key = (RENAME[link][block], quarter)
            found.setdefault(key, []).append((numbers[link, i], at, size))
    return found


NT = (((1,), (1,)), ((), ()))


def dot_nt(a, b):
    return lax.dot_general(a, b, NT, preferred_element_type=F32)


def dot(a, b):
    return jnp.dot(a, b, preferred_element_type=F32)


def kernel(
    len_ref,
    q_hbm,
    rk_hbm,
    rv_hbm,
    pk_hbm,
    pv_hbm,
    up_ref,
    wq_hbm,
    wk_hbm,
    wv_hbm,
    wo_hbm,
    out_ref,
    pg_ref,
    blocks,
    wo,
    wc,
    q,
    kv,
    kt,
    vt,
    scores,
    prob,
    out_t,
    go_acc,
    inv,
    go,
    delta,
    ds,
    dq_t,
    dkv,
    grads,
    landed,
    p_send,
    p_land,
    p_land_z,
    p_land_h,
    load_sem,
    gs_sem,
    gr_sem,
    rs_sem,
    rr_sem,
    ps_sem,
    pr_sem,
):
    r = lax.axis_index("resp")
    t = lax.axis_index("tp")
    z, xh, core = r // 4, (r // 2) % 2, r % 2
    xl, y = t // 4, t % 4
    up1, down1, far1 = (y + 1) % 4, (y + 3) % 4, (y + 2) % 4
    own, other = xl * 4, (1 - xl) * 4
    ids = [t, own + up1, own + down1, other + y, own + far1, other + up1, other + down1, other + far1]
    device = {"X": (r, ids[3]), "U": (r, ids[1]), "D": (r, ids[2])}
    dev_s = (z * 4 + xh * 2 + 1 - core, t)
    dev_h = (z * 4 + (1 - xh) * 2 + core, t)
    dev_z = [(((z + k) % 4) * 4 + xh * 2 + core, t) for k in (1, 2, 3)]

    barrier = pltpu.get_barrier_semaphore()
    peers = list(device.values()) + [dev_s, dev_h] + dev_z
    for peer in peers:
        pl.semaphore_signal(barrier, inc=1, device_id=peer, device_id_type=MESH)

    loads = []

    def load(src, dst):
        copy = pltpu.make_async_copy(src, dst, load_sem.at[len(loads)])
        copy.start()
        loads.append(copy)
        return copy

    my_slot = core * 8 + z * 2 + xh
    own_prompt = [
        load(pk_hbm, kv.at[my_slot, :, 0:HEAD]),
        load(pv_hbm, kv.at[my_slot, :, HEAD : 2 * HEAD]),
    ]
    own_q = [
        load(
            q_hbm.at[0, pl.ds(pl.multiple_of(ids[p] * ROWS, ROWS), ROWS)],
            grads.at[pl.ds(p * ROWS, ROWS), 0:640],
        )
        for p in range(8)
    ]
    own_keys = []
    for i in range(8):
        rows = pl.ds(i * ROWS, ROWS)
        own_keys.append(load(rk_hbm.at[0, rows], kv.at[16 + i, :, 0:HEAD]))
        own_keys.append(load(rv_hbm.at[0, rows], kv.at[16 + i, :, HEAD : 2 * HEAD]))

    position = t * ROWS + lax.broadcasted_iota(jnp.int32, (ROWS, WIDTH), 0)
    live = position < len_ref[0]
    blocks[0] = jnp.where(live, up_ref[0], jnp.zeros((), BF))

    pl.semaphore_wait(barrier, len(peers))

    def p_copy(k, src, dst, dev):
        return pltpu.make_async_remote_copy(
            src_ref=src, dst_ref=dst, send_sem=ps_sem.at[k], recv_sem=pr_sem.at[k],
            device_id=dev, device_id_type=MESH,
        )

    def p_recv(k, dst, dev):
        p_copy(k, dst, dst, dev).wait_recv()

    for copy in own_prompt:
        copy.wait()
    to_h = p_copy(0, kv.at[my_slot], kv.at[my_slot], dev_h)
    to_h.start()

    g_number, g_arrive = number(GATHER), arrivals(GATHER)
    g_sent, g_seen, g_next = [], set(), {link: 0 for link in LINKS}

    def g_copy(k, src_name, dst_name, quarter, at, size, dev):
        cols = pl.ds(quarter * QUARTER + at, size)
        return pltpu.make_async_remote_copy(
            src_ref=blocks.at[POS[src_name], :, cols],
            dst_ref=blocks.at[POS[dst_name], :, cols],
            send_sem=gs_sem.at[k], recv_sem=gr_sem.at[k], device_id=dev, device_id_type=MESH,
        )

    def g_have(name, quarters=(0, 1, 2, 3)):
        for quarter in quarters:
            if name == "o" or (name, quarter) in g_seen:
                continue
            g_seen.add((name, quarter))
            for k, at, size in g_arrive[name, quarter]:
                g_copy(k, name, name, quarter, at, size, device["X"]).wait_recv()

    def g_send(link, count):
        for _ in range(count):
            i = g_next[link]
            g_next[link] = i + 1
            name, quarter, at, size = GATHER[link][i]
            g_have(name, (quarter,))
            copy = g_copy(
                g_number[link, i], name, RENAME[link][name], quarter, at, size, device[link]
            )
            copy.start()
            g_sent.append(copy)

    for _ in range(4):
        for link in LINKS:
            g_send(link, 1)

    wo_load = load(wo_hbm, wo)
    wc_loads = [
        load(wq_hbm, wc.at[:, 0:640]),
        load(wk_hbm, wc.at[:, 640:768]),
        load(wv_hbm, wc.at[:, 768:896]),
    ]
    p_recv(0, kv.at[core * 8 + z * 2 + 1 - xh], dev_h)
    to_z = []
    for k in range(3):
        pair = kv.at[pl.ds(core * 8 + z * 2, 2)]
        copy = p_copy(1 + k, pair, pair, dev_z[k])
        copy.start()
        to_z.append(copy)
    dkv[...] = jnp.zeros_like(dkv)
    for copy in own_q:
        copy.wait()
    for s in range(4):
        for h in range(HEADS):
            q[s, h] = grads[s * SUB : (s + 1) * SUB, h * HEAD : (h + 1) * HEAD]
    for copy in own_keys:
        copy.wait()

    def keys_of(c):
        return kv[pl.ds(c * 4, 4), :, 0:HEAD].reshape(CHUNK, HEAD)

    def values_of(c):
        return kv[pl.ds(c * 4, 4), :, HEAD : 2 * HEAD].reshape(CHUNK, HEAD)

    def flip(c, _):
        kt[c] = keys_of(c).astype(F32).T.astype(BF)
        vt[c] = values_of(c).astype(F32).T.astype(BF)
        return 0

    lax.fori_loop(4, 6, flip, 0)
    for k in range(3):
        p_recv(1 + k, kv.at[pl.ds(core * 8 + ((z + 3 - k) % 4) * 2, 2)], dev_z[k])
    lane_half = kv.at[pl.ds(core * 8, 8)]
    to_s = p_copy(4, lane_half, lane_half, dev_s)
    to_s.start()
    p_recv(4, kv.at[pl.ds((1 - core) * 8, 8)], dev_s)
    lax.fori_loop(0, 4, flip, 0)

    scaling = 1.0 / math.sqrt(HEAD)
    to_log2 = scaling * math.log2(math.e)

    def softmax(s):
        lane = lax.broadcasted_iota(jnp.int32, (1, SUB), 1)
        row = jnp.where(lane < ROWS, ids[2 * s] * ROWS, ids[2 * s + 1] * ROWS - ROWS) + lane
        q_rows = q[s].reshape(LANES, HEAD)

        def first(c, tops):
            key_at = (c - 4) * CHUNK + lax.broadcasted_iota(jnp.int32, (CHUNK, SUB), 0)
            seen = key_at <= row
            all_heads = dot_nt(keys_of(c), q_rows)
            new = []
            for h in range(HEADS):
                lanes = slice(h * SUB, (h + 1) * SUB)
                part = jnp.where(seen, all_heads[:, lanes], -1e30)
                scores[c, :, lanes] = part
                new.append(jnp.maximum(tops[h], jnp.max(part, axis=0, keepdims=True)))
            return tuple(new)

        tops = lax.fori_loop(
            0, 6, first, tuple(jnp.full((1, SUB), -1e30, F32) for _ in range(HEADS)), unroll=3
        )
        out_t[s] = jnp.zeros((HEAD, LANES), F32)

        def second(c, sums):
            new = []
            for h in range(HEADS):
                lanes = slice(h * SUB, (h + 1) * SUB)
                e = jnp.exp2((scores[c, :, lanes] - tops[h]) * to_log2)
                prob[s, c, :, lanes] = e.astype(BF)
                new.append(sums[h] + jnp.sum(e, axis=0, keepdims=True))
            out_t[s] += dot(vt[c], prob[s, c])
            return tuple(new)

        sums = lax.fori_loop(
            0, 6, second, tuple(jnp.zeros((1, SUB), F32) for _ in range(HEADS)), unroll=3
        )
        for h in range(HEADS):
            lanes = slice(h * SUB, (h + 1) * SUB)
            inverse = 1.0 / sums[h]
            out_t[s, :, lanes] = out_t[s, :, lanes] * inverse
            inv[s, h] = jnp.broadcast_to(inverse, (SUB, HEAD)).T

    def project(subs):
        first, count = subs[0], len(subs)
        rows = count * SUB
        for at, size in ((0, 256), (256, 256), (512, 128)):
            part = blocks[2 * first : 2 * (first + count)].reshape(rows, WIDTH)
            go_acc[first * SUB : first * SUB + rows, at : at + size] = dot_nt(
                part, wo[at : at + size, :]
            )

    def project_part(s, quarter, start):
        cols = slice(quarter * QUARTER, (quarter + 1) * QUARTER)
        rows = slice(s * SUB, (s + 1) * SUB)
        part = dot_nt(blocks[2 * s : 2 * s + 2, :, cols].reshape(SUB, QUARTER), wo[:, cols])
        if start:
            go_acc[rows] = part
        else:
            go_acc[rows] += part

    def attend(subs):
        first, count = subs[0], len(subs)
        for s in subs:
            for h in range(HEADS):
                lanes = slice(h * SUB, (h + 1) * SUB)
                part = go_acc[s * SUB : (s + 1) * SUB, h * HEAD : (h + 1) * HEAD] * inv[s, h]
                go[s, h] = part.astype(BF)
                delta[s, 0:1, lanes] = jnp.sum(
                    part.T * out_t[s, :, lanes], axis=0, keepdims=True
                )
        wide = count * LANES
        dq_t[:, 0:wide] = jnp.zeros((HEAD, wide), F32)

        def step(c, _):
            values = values_of(c)
            dv = None
            for j, s in enumerate(subs):
                dp = dot_nt(values, go[s].reshape(LANES, HEAD))
                for h in range(HEADS):
                    lanes = slice(h * SUB, (h + 1) * SUB)
                    e = prob[s, c, :, lanes].astype(F32)
                    ds[:, j * LANES + h * SUB : j * LANES + (h + 1) * SUB] = (
                        e * (dp[:, lanes] - delta[s, 0:1, lanes])
                    ).astype(BF)
                part = dot(prob[s, c], go[s].reshape(LANES, HEAD))
                dv = part if dv is None else dv + part
            dk = dot(ds[:, 0:wide], q[first : first + count].reshape(wide, HEAD))
            dkv[pl.ds(c * 4, 4), :, 0:HEAD] += dk.reshape(4, ROWS, HEAD)
            dkv[pl.ds(c * 4, 4), :, HEAD : 2 * HEAD] += dv.reshape(4, ROWS, HEAD)
            dq_t[:, 0:wide] += dot(kt[c], ds[:, 0:wide])
            return 0

        lax.fori_loop(0, 6, step, 0, unroll=3)
        for j, s in enumerate(subs):
            for h in range(HEADS):
                at = j * LANES + h * SUB
                grads[s * SUB : (s + 1) * SUB, h * HEAD : (h + 1) * HEAD] = (
                    (dq_t[:, at : at + SUB] * scaling).T.astype(BF)
                )

    for link in ("U", "D"):
        g_send(link, 3)
    g_send("X", 2)
    softmax(0)
    softmax(1)
    wo_load.wait()
    for link in LINKS:
        g_send(link, 2)
    for name in ("U", "D", "X"):
        g_have(name)
    project((0, 1))
    attend((0, 1))
    softmax(2)
    for link in LINKS:
        g_send(link, 1)
    softmax(3)
    g_send("X", 1)
    for n, quarter in enumerate((0, 1, 2, 3)):
        g_have("F", (quarter,))
        g_have("XU", (quarter,))
        project_part(2, quarter, n == 0)
    attend((2,))
    for n, quarter in enumerate((0, 2, 3, 1)):
        g_have("XD", (quarter,))
        g_have("XF", (quarter,))
        project_part(3, quarter, n == 0)
    attend((3,))
    for copy in g_sent:
        copy.wait_send()
    to_h.wait_send()
    for copy in to_z:
        copy.wait_send()
    to_s.wait_send()

    dkv_scale = jnp.where(
        lax.broadcasted_iota(jnp.int32, (1, 1, 2 * HEAD), 2) < HEAD, scaling, 1.0
    ).astype(F32)
    for p in range(8):
        grads[p * ROWS : (p + 1) * ROWS, 640:896] = (dkv[16 + ids[p]] * dkv_scale[0]).astype(BF)
    for copy in wc_loads:
        copy.wait()

    r_number, r_arrive = number(REDUCE), arrivals(REDUCE)
    r_sent, r_seen, r_next = [], set(), {link: 0 for link in LINKS}

    def r_copy(k, src, size, dev):
        return pltpu.make_async_remote_copy(
            src_ref=src, dst_ref=landed.at[k, :, pl.ds(0, size)],
            send_sem=rs_sem.at[k], recv_sem=rr_sem.at[k], device_id=dev, device_id_type=MESH,
        )

    def r_wait(k, size):
        r_copy(k, landed.at[k, :, pl.ds(0, size)], size, device["X"]).wait_recv()

    def r_add(name, quarter):
        if (name, quarter) in r_seen:
            return
        r_seen.add((name, quarter))
        for k, at, size in r_arrive.get((name, quarter), ()):
            r_wait(k, size)
            cols = pl.ds(quarter * QUARTER + at, size)
            mine = blocks[POS[name], :, cols].astype(F32)
            blocks[POS[name], :, cols] = (mine + landed[k, :, 0:size].astype(F32)).astype(BF)

    def r_send(link, count):
        for _ in range(count):
            i = r_next[link]
            r_next[link] = i + 1
            name, quarter, at, size = REDUCE[link][i]
            r_add(name, quarter)
            k = r_number[link, i]
            src = blocks.at[POS[name], :, pl.ds(quarter * QUARTER + at, size)]
            copy = r_copy(k, src, size, device[link])
            copy.start()
            r_sent.append(copy)

    def term(half, quarter):
        rows = slice(half * 256, half * 256 + 256)
        for k in range(5):
            start = quarter * QUARTER + k * 256
            value = dot_nt(grads[rows, :], wc[start : start + 256, :]).astype(BF)
            blocks[half * 4 : half * 4 + 4, :, start : start + 256] = value.reshape(4, ROWS, 256)

    term(1, 1)
    r_send("X", 3)
    term(1, 3)
    r_send("U", 2)
    r_send("D", 1)
    term(1, 2)
    r_send("U", 2)
    r_send("D", 1)
    term(1, 0)
    r_send("X", 3)
    r_send("U", 1)
    p_send[...] = (dkv[pl.ds((1 - core) * 8, 8)] * dkv_scale).astype(BF)
    ps = p_copy(5, p_send, p_land, dev_s)
    ps.start()
    term(0, 3)
    r_send("D", 1)
    term(0, 2)
    r_send("D", 2)
    term(0, 1)
    r_send("X", 1)
    r_send("D", 1)
    term(0, 0)

    ps.wait_send()
    p_recv(5, p_land, dev_s)
    mine = pl.ds(core * 8, 8)
    dkv[mine] = dkv[mine] * dkv_scale + p_land[...].astype(F32)
    p_send[...] = dkv[mine].astype(BF)
    z_copies = []
    for k in range(3):
        peer_z = (z + 1 + k) % 4
        copy = p_copy(6 + k, p_send.at[pl.ds(peer_z * 2, 2)], p_land_z.at[k], dev_z[k])
        copy.start()
        z_copies.append(copy)

    r_send("U", 2)

    for k in range(3):
        z_copies[k].wait_send()
        p_recv(6 + k, p_land_z.at[k], dev_z[k])
    pair_at = core * 8 + z * 2
    both = dkv[pl.ds(pair_at, 2)]
    for k in range(3):
        both = both + p_land_z[k].astype(F32)
    dkv[pl.ds(pair_at, 2)] = both
    p_send[0] = dkv[pair_at + 1 - xh].astype(BF)
    ph = p_copy(9, p_send.at[0], p_land_h, dev_h)
    ph.start()

    r_send("D", 2)
    r_send("U", 3)
    p_recv(9, p_land_h, dev_h)
    pg_ref[...] = dkv[pair_at + xh] + p_land_h[...].astype(F32)
    r_send("X", 2)
    r_send("D", 2)
    r_send("X", 1)
    ph.wait_send()

    for quarter in (0, 1, 2, 3):
        cols = slice(quarter * QUARTER, (quarter + 1) * QUARTER)
        total = blocks[0, :, cols].astype(F32)
        for k, at, size in r_arrive["o", quarter]:
            r_wait(k, size)
            total = total + landed[k].astype(F32)
        out_ref[0, :, cols] = total.astype(BF)
    for copy in r_sent:
        copy.wait_send()


def split_kernel(rows_ref, both_ref, out_ref, key_ref, value_ref):
    out_ref[...] = rows_ref[...]
    key_ref[...] = both_ref[:, 0:HEAD]
    value_ref[...] = both_ref[:, HEAD : 2 * HEAD]


def split(input_grad, prompt_grads):
    vmem = pl.BlockSpec(memory_space=pltpu.VMEM)
    return pl.pallas_call(
        split_kernel,
        out_shape=(
            jax.ShapeDtypeStruct((1, ROWS, WIDTH), BF),
            jax.ShapeDtypeStruct((ROWS, HEAD), F32),
            jax.ShapeDtypeStruct((ROWS, HEAD), F32),
        ),
        in_specs=[vmem, vmem],
        out_specs=(vmem, vmem, vmem),
    )(input_grad, prompt_grads)


def body(
    queries,
    response_keys,
    response_values,
    prompt_key_rows,
    prompt_value_rows,
    upstream,
    lengths,
    query_weight,
    key_matrix,
    value_matrix,
    out_weight,
):
    vmem = pl.BlockSpec(memory_space=pltpu.VMEM)
    smem = pl.BlockSpec(memory_space=pltpu.SMEM)
    hbm = pl.BlockSpec(memory_space=pl.ANY)
    dma = pltpu.SemaphoreType.DMA
    input_grad, prompt_grads = pl.pallas_call(
        kernel,
        out_shape=(
            jax.ShapeDtypeStruct((1, ROWS, WIDTH), BF),
            jax.ShapeDtypeStruct((ROWS, 2 * HEAD), F32),
        ),
        in_specs=[smem, hbm, hbm, hbm, hbm, hbm, vmem, hbm, hbm, hbm, hbm],
        out_specs=(vmem, vmem),
        scratch_shapes=[
            pltpu.VMEM((8, ROWS, WIDTH), BF),
            pltpu.VMEM((HEADS * HEAD, WIDTH), BF),
            pltpu.VMEM((WIDTH, 896), BF),
            pltpu.VMEM((4, HEADS, SUB, HEAD), BF),
            pltpu.VMEM((24, ROWS, 2 * HEAD), BF),
            pltpu.VMEM((6, HEAD, CHUNK), BF),
            pltpu.VMEM((6, HEAD, CHUNK), BF),
            pltpu.VMEM((6, CHUNK, LANES), F32),
            pltpu.VMEM((4, 6, CHUNK, LANES), BF),
            pltpu.VMEM((4, HEAD, LANES), F32),
            pltpu.VMEM((4 * SUB, HEADS * HEAD), F32),
            pltpu.VMEM((4, HEADS, SUB, HEAD), F32),
            pltpu.VMEM((4, HEADS, SUB, HEAD), BF),
            pltpu.VMEM((4, 8, LANES), F32),
            pltpu.VMEM((CHUNK, 2 * LANES), BF),
            pltpu.VMEM((HEAD, 2 * LANES), F32),
            pltpu.VMEM((24, ROWS, 2 * HEAD), F32),
            pltpu.VMEM((8 * ROWS, 896), BF),
            pltpu.VMEM((30, ROWS, QUARTER), BF),
            pltpu.VMEM((8, ROWS, 2 * HEAD), BF),
            pltpu.VMEM((8, ROWS, 2 * HEAD), BF),
            pltpu.VMEM((3, 2, ROWS, 2 * HEAD), BF),
            pltpu.VMEM((ROWS, 2 * HEAD), BF),
            dma((32,)),
            dma((30,)),
            dma((30,)),
            dma((30,)),
            dma((30,)),
            dma((10,)),
            dma((10,)),
        ],
        compiler_params=pltpu.CompilerParams(
            collective_id=0, has_side_effects=True, vmem_limit_bytes=62 * 1024 * 1024
        ),
        cost_estimate=pl.CostEstimate(
            flops=18_000_000_000, bytes_accessed=20_000_000, transcendentals=4_000_000
        ),
    )(
        lengths,
        queries,
        response_keys,
        response_values,
        prompt_key_rows,
        prompt_value_rows,
        upstream,
        query_weight,
        key_matrix,
        value_matrix,
        out_weight,
    )
    return split(input_grad, prompt_grads)


def solution(mesh):
    in_specs = (
        P("resp", None, "tp"),
        P("resp", None, "tp"),
        P("resp", None, "tp"),
        P("resp", "tp"),
        P("resp", "tp"),
        P("resp", "tp", None),
        P("resp"),
        P(None, "tp"),
        P(None, "tp"),
        P(None, "tp"),
        P("tp", None),
    )
    out_specs = (P("resp", "tp", None), P("resp", "tp"), P("resp", "tp"))
    return jax.shard_map(body, mesh=mesh, in_specs=in_specs, out_specs=out_specs, check_vma=False)
```

```python
import functools
import math

import jax
import jax.numpy as jnp
from jax import lax
from jax.experimental import pallas as pl
from jax.experimental.pallas import tpu as pltpu
from jax.sharding import PartitionSpec as P

MESH = pl.DeviceIdType.MESH
BF = jnp.bfloat16
F32 = jnp.float32
WIDTH = 5120
HEADS = 5
HEAD = 128
ROWS = 64
SUB = 128
CHUNK = 256
LANES = HEADS * SUB
QUARTER = WIDTH // 4

ORDER = ("o", "U", "D", "X", "F", "XU", "XD", "XF")
POS = {name: i for i, name in enumerate(ORDER)}
RENAME = {
    "X": {"o": "X", "D": "XD", "U": "XU", "F": "XF", "X": "o", "XU": "U", "XD": "D", "XF": "F"},
    "U": {"o": "D", "D": "F", "X": "XD", "XD": "XF", "F": "U", "XF": "XU", "U": "o", "XU": "X"},
    "D": {"o": "U", "U": "F", "X": "XU", "XU": "XF", "F": "D", "XF": "XD", "D": "o", "XD": "X"},
}
Q = QUARTER
A = 896
B = Q - A
GATHER = {
    "X": (("o", 3, 0, Q), ("o", 2, 0, Q), ("o", 1, 0, Q), ("o", 0, 0, Q), ("D", 0, 0, A), ("D", 1, 0, Q),
          ("U", 0, 0, A), ("U", 1, 0, Q), ("F", 0, 0, Q), ("F", 1, 0, Q)),
    "U": (("o", 0, 0, Q), ("o", 1, 0, Q), ("o", 2, 0, Q), ("o", 3, 0, Q), ("X", 3, 0, Q), ("D", 0, 0, Q),
          ("D", 1, 0, Q), ("X", 0, A, B), ("X", 2, 0, Q), ("XD", 3, 0, Q)),
    "D": (("o", 2, 0, Q), ("o", 3, 0, Q), ("o", 0, 0, Q), ("o", 1, 0, Q), ("X", 2, 0, Q), ("U", 2, 0, Q),
          ("U", 3, 0, Q), ("X", 0, A, B), ("X", 3, 0, Q), ("XU", 2, 0, Q)),
}
A2 = 1024
B2 = Q - A2
REDUCE = {
    "X": (("X", 1, 0, 512), ("X", 1, 512, 768), ("XU", 1, 0, Q), ("XF", 1, 0, Q), ("XD", 1, 0, Q), ("XF", 0, 0, Q),
          ("XU", 0, 0, A2), ("XD", 0, 0, A2), ("X", 2, 0, Q), ("X", 0, 0, Q), ("X", 3, 0, Q)),
    "U": (("XU", 3, 0, Q), ("F", 3, 0, Q), ("XF", 2, 0, Q), ("F", 2, 0, Q), ("XU", 0, A2, B2), ("XU", 2, 0, Q),
          ("U", 1, 0, Q), ("U", 0, 0, Q), ("U", 3, 0, Q), ("U", 2, 0, Q)),
    "D": (("D", 3, 0, Q), ("XF", 3, 0, Q), ("XD", 2, 0, Q), ("D", 2, 0, Q), ("XD", 0, A2, B2), ("F", 1, 0, Q),
          ("F", 0, 0, Q), ("XD", 3, 0, Q), ("D", 1, 0, Q), ("D", 0, 0, Q)),
}
LINKS = ("X", "U", "D")


def number(plan):
    keys = [(link, i) for link in LINKS for i in range(len(plan[link]))]
    return {key: n for n, key in enumerate(keys)}


def arrivals(plan):
    found = {}
    numbers = number(plan)
    for i in range(max(len(pieces) for pieces in plan.values())):
        for link in LINKS:
            if i >= len(plan[link]):
                continue
            block, quarter, at, size = plan[link][i]
            key = (RENAME[link][block], quarter)
            found.setdefault(key, []).append((numbers[link, i], at, size))
    return found


NT = (((1,), (1,)), ((), ()))


def dot_nt(a, b):
    return lax.dot_general(a, b, NT, preferred_element_type=F32)


def dot(a, b):
    return jnp.dot(a, b, preferred_element_type=F32)


def kernel(
    len_ref,
    q_hbm,
    rk_hbm,
    rv_hbm,
    pk_hbm,
    pv_hbm,
    up_hbm,
    wq_hbm,
    wk_hbm,
    wv_hbm,
    wo_hbm,
    out_hbm,
    pg_ref,
    blocks,
    wo,
    wc,
    q,
    kv,
    kt,
    vt,
    scores,
    prob,
    out_t,
    go_acc,
    inv,
    go,
    delta,
    ds,
    dq_t,
    dkv,
    grads,
    landed,
    p_send,
    p_land,
    p_land_z,
    p_land_h,
    load_sem,
    store_sem,
    gs_sem,
    gr_sem,
    rs_sem,
    rr_sem,
    ps_sem,
    pr_sem,
):
    r = lax.axis_index("resp")
    t = lax.axis_index("tp")
    z, xh, core = r // 4, (r // 2) % 2, r % 2
    xl, y = t // 4, t % 4
    up1, down1, far1 = (y + 1) % 4, (y + 3) % 4, (y + 2) % 4
    own, other = xl * 4, (1 - xl) * 4
    ids = [t, own + up1, own + down1, other + y, own + far1, other + up1, other + down1, other + far1]
    device = {"X": (r, ids[3]), "U": (r, ids[1]), "D": (r, ids[2])}
    dev_s = (z * 4 + xh * 2 + 1 - core, t)
    dev_h = (z * 4 + (1 - xh) * 2 + core, t)
    dev_z = [(((z + k) % 4) * 4 + xh * 2 + core, t) for k in (1, 2, 3)]

    barrier = pltpu.get_barrier_semaphore()
    peers = list(device.values()) + [dev_s, dev_h] + dev_z
    for peer in peers:
        pl.semaphore_signal(barrier, inc=1, device_id=peer, device_id_type=MESH)

    loads = []

    def load(src, dst):
        copy = pltpu.make_async_copy(src, dst, load_sem.at[len(loads)])
        copy.start()
        loads.append(copy)
        return copy

    my_slot = core * 8 + z * 2 + xh
    own_prompt = [
        load(pk_hbm, kv.at[my_slot, :, 0:HEAD]),
        load(pv_hbm, kv.at[my_slot, :, HEAD : 2 * HEAD]),
    ]
    own_rows = {}
    for n in (3, 0, 2, 1):
        cols = pl.ds(n * QUARTER, QUARTER)
        own_rows[n] = load(up_hbm.at[0, :, cols], blocks.at[0, :, cols])
    for copy in own_prompt + list(own_rows.values()):
        copy.wait()
    pl.semaphore_wait(barrier, len(peers))

    def p_copy(k, src, dst, dev):
        return pltpu.make_async_remote_copy(
            src_ref=src, dst_ref=dst, send_sem=ps_sem.at[k], recv_sem=pr_sem.at[k],
            device_id=dev, device_id_type=MESH,
        )

    def p_recv(k, dst, dev):
        p_copy(k, dst, dst, dev).wait_recv()


    to_h = p_copy(0, kv.at[my_slot], kv.at[my_slot], dev_h)
    to_h.start()

    g_number, g_arrive = number(GATHER), arrivals(GATHER)
    g_sent, g_seen, g_next = [], set(), {link: 0 for link in LINKS}

    def g_copy(k, src_name, dst_name, quarter, at, size, dev):
        cols = pl.ds(quarter * QUARTER + at, size)
        return pltpu.make_async_remote_copy(
            src_ref=blocks.at[POS[src_name], :, cols],
            dst_ref=blocks.at[POS[dst_name], :, cols],
            send_sem=gs_sem.at[k], recv_sem=gr_sem.at[k], device_id=dev, device_id_type=MESH,
        )

    def g_have(name, quarters=(0, 1, 2, 3)):
        for quarter in quarters:
            if name == "o" or (name, quarter) in g_seen:
                continue
            g_seen.add((name, quarter))
            for k, at, size in g_arrive[name, quarter]:
                g_copy(k, name, name, quarter, at, size, device["X"]).wait_recv()

    def g_send(link, count):
        for _ in range(count):
            i = g_next[link]
            g_next[link] = i + 1
            name, quarter, at, size = GATHER[link][i]
            g_have(name, (quarter,))
            copy = g_copy(
                g_number[link, i], name, RENAME[link][name], quarter, at, size, device[link]
            )
            copy.start()
            g_sent.append(copy)

    for link in LINKS:
        g_send(link, 1)
    for _ in range(3):
        for link in LINKS:
            g_send(link, 1)

    own_q = [
        load(
            q_hbm.at[0, pl.ds(pl.multiple_of(ids[p] * ROWS, ROWS), ROWS)],
            grads.at[pl.ds(p * ROWS, ROWS), 0:640],
        )
        for p in range(8)
    ]
    own_keys = []
    for i in range(8):
        rows = pl.ds(i * ROWS, ROWS)
        own_keys.append(load(rk_hbm.at[0, rows], kv.at[16 + i, :, 0:HEAD]))
        own_keys.append(load(rv_hbm.at[0, rows], kv.at[16 + i, :, HEAD : 2 * HEAD]))
    wo_load = load(wo_hbm, wo)
    wc_loads = [
        load(wq_hbm, wc.at[:, 0:640]),
        load(wk_hbm, wc.at[:, 640:768]),
        load(wv_hbm, wc.at[:, 768:896]),
    ]
    p_recv(0, kv.at[core * 8 + z * 2 + 1 - xh], dev_h)
    to_z, to_s = [], []
    for k in range(3):
        pair = kv.at[pl.ds(core * 8 + z * 2, 2)]
        copy = p_copy(1 + k, pair, pair, dev_z[k])
        copy.start()
        to_z.append(copy)

    def to_other_core(k, at_z):
        pair = kv.at[pl.ds(core * 8 + at_z * 2, 2)]
        copy = p_copy(k, pair, pair, dev_s)
        copy.start()
        to_s.append(copy)

    to_other_core(4, z)
    dkv[...] = jnp.zeros_like(dkv)
    for copy in own_q:
        copy.wait()
    for s in range(4):
        for h in range(HEADS):
            q[s, h] = grads[s * SUB : (s + 1) * SUB, h * HEAD : (h + 1) * HEAD]
    for copy in own_keys:
        copy.wait()

    def keys_of(c):
        return kv[pl.ds(c * 4, 4), :, 0:HEAD].reshape(CHUNK, HEAD)

    def values_of(c):
        return kv[pl.ds(c * 4, 4), :, HEAD : 2 * HEAD].reshape(CHUNK, HEAD)

    def flip(c, _):
        kt[c] = keys_of(c).astype(F32).T.astype(BF)
        vt[c] = values_of(c).astype(F32).T.astype(BF)
        return 0

    scaling = 1.0 / math.sqrt(HEAD)
    to_log2 = scaling * math.log2(math.e)

    def rows_of(s):
        lane = lax.broadcasted_iota(jnp.int32, (1, SUB), 1)
        return jnp.where(lane < ROWS, ids[2 * s] * ROWS, ids[2 * s + 1] * ROWS - ROWS) + lane

    no_tops = tuple(jnp.full((1, SUB), -1e30, F32) for _ in range(HEADS))

    def score(s, low, count, tops):
        row = rows_of(s)
        q_rows = q[s].reshape(LANES, HEAD)

        def first(i, tops):
            c = low + i
            key_at = (c - 4) * CHUNK + lax.broadcasted_iota(jnp.int32, (CHUNK, SUB), 0)
            seen = key_at <= row
            all_heads = dot_nt(keys_of(c), q_rows)
            new = []
            for h in range(HEADS):
                lanes = slice(h * SUB, (h + 1) * SUB)
                part = jnp.where(seen, all_heads[:, lanes], -1e30)
                scores[s % 2, c, :, lanes] = part
                new.append(jnp.maximum(tops[h], jnp.max(part, axis=0, keepdims=True)))
            return tuple(new)

        return lax.fori_loop(0, count, first, tops, unroll=min(count, 3))

    def softmax(s, tops):
        row = rows_of(s)
        out_t[s] = jnp.zeros((HEAD, LANES), F32)

        def second(c, sums):
            new = []
            for h in range(HEADS):
                lanes = slice(h * SUB, (h + 1) * SUB)
                e = jnp.exp2((scores[s % 2, c, :, lanes] - tops[h]) * to_log2)
                prob[s, c, :, lanes] = e.astype(BF)
                new.append(sums[h] + jnp.sum(e, axis=0, keepdims=True))
            out_t[s] += dot(vt[c], prob[s, c])
            return tuple(new)

        sums = lax.fori_loop(
            0, 6, second, tuple(jnp.zeros((1, SUB), F32) for _ in range(HEADS)), unroll=3
        )
        for h in range(HEADS):
            lanes = slice(h * SUB, (h + 1) * SUB)
            inverse = jnp.where(row < len_ref[0], 1.0 / sums[h], 0.0)
            out_t[s, :, lanes] = out_t[s, :, lanes] * inverse
            inv[s, h] = jnp.broadcast_to(inverse, (SUB, HEAD)).T

    def project(subs):
        first, count = subs[0], len(subs)
        rows = count * SUB
        for at, size in ((0, 256), (256, 256), (512, 128)):
            part = blocks[2 * first : 2 * (first + count)].reshape(rows, WIDTH)
            go_acc[first * SUB : first * SUB + rows, at : at + size] = dot_nt(
                part, wo[at : at + size, :]
            )

    def project_part(s, quarter, start):
        cols = slice(quarter * QUARTER, (quarter + 1) * QUARTER)
        rows = slice(s * SUB, (s + 1) * SUB)
        part = dot_nt(blocks[2 * s : 2 * s + 2, :, cols].reshape(SUB, QUARTER), wo[:, cols])
        if start:
            go_acc[rows] = part
        else:
            go_acc[rows] += part

    def attend_rows(subs):
        first, count = subs[0], len(subs)
        for s in subs:
            for h in range(HEADS):
                lanes = slice(h * SUB, (h + 1) * SUB)
                part = go_acc[s * SUB : (s + 1) * SUB, h * HEAD : (h + 1) * HEAD] * inv[s, h]
                go[s, h] = part.astype(BF)
                delta[s, 0:1, lanes] = jnp.sum(
                    part.T * out_t[s, :, lanes], axis=0, keepdims=True
                )
        wide = count * LANES
        dq_t[:, 0:wide] = jnp.zeros((HEAD, wide), F32)

    def attend_keys(subs, low, high):
        first, count = subs[0], len(subs)
        wide = count * LANES

        def step(c, _):
            values = values_of(c)
            dv = None
            for j, s in enumerate(subs):
                dp = dot_nt(values, go[s].reshape(LANES, HEAD))
                for h in range(HEADS):
                    lanes = slice(h * SUB, (h + 1) * SUB)
                    e = prob[s, c, :, lanes].astype(F32)
                    ds[:, j * LANES + h * SUB : j * LANES + (h + 1) * SUB] = (
                        e * (dp[:, lanes] - delta[s, 0:1, lanes])
                    ).astype(BF)
                part = dot(prob[s, c], go[s].reshape(LANES, HEAD))
                dv = part if dv is None else dv + part
            dk = dot(ds[:, 0:wide], q[first : first + count].reshape(wide, HEAD))
            dkv[pl.ds(c * 4, 4), :, 0:HEAD] += dk.reshape(4, ROWS, HEAD)
            dkv[pl.ds(c * 4, 4), :, HEAD : 2 * HEAD] += dv.reshape(4, ROWS, HEAD)
            dq_t[:, 0:wide] += dot(kt[c], ds[:, 0:wide])
            return 0

        lax.fori_loop(low, high, step, 0, unroll=min(high - low, 3))

    def attend_done(subs):
        for j, s in enumerate(subs):
            for h in range(HEADS):
                at = j * LANES + h * SUB
                grads[s * SUB : (s + 1) * SUB, h * HEAD : (h + 1) * HEAD] = (
                    (dq_t[:, at : at + SUB] * scaling).T.astype(BF)
                )

    def attend(subs):
        attend_rows(subs)
        attend_keys(subs, 0, 6)
        attend_done(subs)

    lax.fori_loop(4, 6, flip, 0)
    tops = [score(s, 4, 2, no_tops) for s in (0, 1)]
    for k in range(3):
        at_z = (z + 3 - k) % 4
        p_recv(1 + k, kv.at[pl.ds(core * 8 + at_z * 2, 2)], dev_z[k])
        to_other_core(5 + k, at_z)
    lax.fori_loop(core * 2, core * 2 + 2, flip, 0)
    tops = [score(s, core * 2, 2, tops[s]) for s in (0, 1)]
    for link in ("U", "D"):
        g_send(link, 3)
    g_send("X", 2)
    for k in range(4):
        at_z = (z + 4 - k) % 4
        p_recv(4 + k, kv.at[pl.ds((1 - core) * 8 + at_z * 2, 2)], dev_s)
    lax.fori_loop((1 - core) * 2, (1 - core) * 2 + 2, flip, 0)
    tops = [score(s, (1 - core) * 2, 2, tops[s]) for s in (0, 1)]
    softmax(0, tops[0])
    softmax(1, tops[1])
    wo_load.wait()
    for link in LINKS:
        g_send(link, 2)
    for name in ("U", "D", "X"):
        g_have(name)
    project((0, 1))
    attend((0, 1))
    softmax(2, score(2, 0, 6, no_tops))
    for link in LINKS:
        g_send(link, 1)
    softmax(3, score(3, 0, 6, no_tops))
    g_send("X", 1)
    for n, quarter in enumerate((0, 1, 2, 3)):
        g_have("F", (quarter,))
        g_have("XU", (quarter,))
        project_part(2, quarter, n == 0)
    attend((2,))
    for n, quarter in enumerate((0, 2, 3, 1)):
        g_have("XD", (quarter,))
        g_have("XF", (quarter,))
        project_part(3, quarter, n == 0)
    attend_rows((3,))
    attend_keys((3,), 4, 6)
    for copy in g_sent:
        copy.wait_send()
    to_h.wait_send()
    for copy in to_z + to_s:
        copy.wait_send()

    dkv_scale = jnp.where(
        lax.broadcasted_iota(jnp.int32, (1, 1, 2 * HEAD), 2) < HEAD, scaling, 1.0
    ).astype(F32)
    for p in range(8):
        grads[p * ROWS : (p + 1) * ROWS, 640:896] = (dkv[16 + ids[p]] * dkv_scale[0]).astype(BF)
    for copy in wc_loads:
        copy.wait()

    r_number, r_arrive = number(REDUCE), arrivals(REDUCE)
    r_sent, r_seen, r_next = [], set(), {link: 0 for link in LINKS}

    def r_copy(k, src, size, dev):
        return pltpu.make_async_remote_copy(
            src_ref=src, dst_ref=landed.at[k, :, pl.ds(0, size)],
            send_sem=rs_sem.at[k], recv_sem=rr_sem.at[k], device_id=dev, device_id_type=MESH,
        )

    def r_wait(k, size):
        r_copy(k, landed.at[k, :, pl.ds(0, size)], size, device["X"]).wait_recv()

    def r_add(name, quarter):
        if (name, quarter) in r_seen:
            return
        r_seen.add((name, quarter))
        for k, at, size in r_arrive.get((name, quarter), ()):
            r_wait(k, size)
            cols = pl.ds(quarter * QUARTER + at, size)
            mine = blocks[POS[name], :, cols].astype(F32)
            blocks[POS[name], :, cols] = (mine + landed[k, :, 0:size].astype(F32)).astype(BF)

    def r_send(link, count):
        for _ in range(count):
            i = r_next[link]
            r_next[link] = i + 1
            name, quarter, at, size = REDUCE[link][i]
            r_add(name, quarter)
            k = r_number[link, i]
            src = blocks.at[POS[name], :, pl.ds(quarter * QUARTER + at, size)]
            copy = r_copy(k, src, size, device[link])
            copy.start()
            r_sent.append(copy)

    def term(low, high, quarter, parts=(0, 1, 2, 3, 4)):
        rows = slice(low * ROWS, high * ROWS)
        for k in parts:
            start = quarter * QUARTER + k * 256
            value = dot_nt(grads[rows, :], wc[start : start + 256, :]).astype(BF)
            blocks[low:high, :, start : start + 256] = value.reshape(high - low, ROWS, 256)

    term(0, 6, 1, (0, 1))
    r_send("X", 1)
    term(0, 6, 1, (2, 3, 4))
    r_send("X", 2)
    term(0, 6, 3)
    r_send("U", 2)
    r_send("D", 1)
    attend_keys((3,), 0, 4)
    attend_done((3,))
    term(6, 8, 3)
    r_send("D", 1)
    term(6, 8, 2)
    r_send("U", 1)
    r_send("D", 1)
    term(6, 8, 1)
    r_send("X", 2)
    term(0, 6, 2)
    r_send("U", 1)
    r_send("D", 1)
    term(6, 8, 0)
    term(0, 6, 0)
    r_send("X", 3)
    r_send("U", 1)
    r_send("D", 1)
    p_send[...] = (dkv[pl.ds((1 - core) * 8, 8)] * dkv_scale).astype(BF)
    ps = p_copy(8, p_send, p_land, dev_s)
    ps.start()
    r_send("D", 1)
    r_send("U", 2)

    ps.wait_send()
    p_recv(8, p_land, dev_s)
    mine = pl.ds(core * 8, 8)
    dkv[mine] = dkv[mine] * dkv_scale + p_land[...].astype(F32)
    p_send[...] = dkv[mine].astype(BF)
    z_copies = []
    for k in range(3):
        peer_z = (z + 1 + k) % 4
        copy = p_copy(9 + k, p_send.at[pl.ds(peer_z * 2, 2)], p_land_z.at[k], dev_z[k])
        copy.start()
        z_copies.append(copy)

    r_send("D", 2)
    r_send("U", 3)

    for k in range(3):
        z_copies[k].wait_send()
        p_recv(9 + k, p_land_z.at[k], dev_z[k])
    pair_at = core * 8 + z * 2
    both = dkv[pl.ds(pair_at, 2)]
    for k in range(3):
        both = both + p_land_z[k].astype(F32)
    dkv[pl.ds(pair_at, 2)] = both
    p_send[0] = dkv[pair_at + 1 - xh].astype(BF)
    ph = p_copy(12, p_send.at[0], p_land_h, dev_h)
    ph.start()

    r_send("X", 2)
    r_send("D", 2)
    r_send("X", 1)
    p_recv(12, p_land_h, dev_h)
    pg_ref[...] = dkv[pair_at + xh] + p_land_h[...].astype(F32)
    to_h_sent = [ph]

    stores = []
    for n, quarter in enumerate((1, 3, 0, 2)):
        cols = pl.ds(quarter * QUARTER, QUARTER)
        total = blocks[0, :, cols].astype(F32)
        strips = []
        for k, at, size in r_arrive["o", quarter]:
            r_wait(k, size)
            if size == QUARTER:
                total = total + landed[k].astype(F32)
            else:
                strips.append((at, landed[k, :, 0:size].astype(F32)))
        if strips:
            strips.sort(key=lambda strip: strip[0])
            total = total + jnp.concatenate([strip[1] for strip in strips], axis=1)
        blocks[0, :, cols] = total.astype(BF)
        copy = pltpu.make_async_copy(blocks.at[0, :, cols], out_hbm.at[0, :, cols], store_sem.at[n])
        copy.start()
        stores.append(copy)
    for copy in r_sent + to_h_sent:
        copy.wait_send()
    for copy in stores:
        copy.wait()


def split_kernel(rows_hbm, both_hbm, out_hbm, key_hbm, value_hbm, rows, both, in_sem, out_sem):
    parts = []
    for n in range(4):
        at = pl.ds(n * 16, 16)
        parts.append((rows_hbm.at[0, at], rows.at[at], ((rows.at[at], out_hbm.at[0, at]),)))
    key, value = both.at[:, 0:HEAD], both.at[:, HEAD : 2 * HEAD]
    parts.append((both_hbm, both, ((key, key_hbm), (value, value_hbm))))
    reads = [pltpu.make_async_copy(p[0], p[1], in_sem.at[n]) for n, p in enumerate(parts)]
    for copy in reads:
        copy.start()
    writes = []
    for read, part in zip(reads, parts):
        read.wait()
        for src, dst in part[2]:
            copy = pltpu.make_async_copy(src, dst, out_sem.at[len(writes)])
            copy.start()
            writes.append(copy)
    for copy in writes:
        copy.wait()


def split(input_grad, prompt_grads):
    hbm = pl.BlockSpec(memory_space=pl.ANY)
    return pl.pallas_call(
        split_kernel,
        out_shape=(
            jax.ShapeDtypeStruct((1, ROWS, WIDTH), BF),
            jax.ShapeDtypeStruct((ROWS, HEAD), F32),
            jax.ShapeDtypeStruct((ROWS, HEAD), F32),
        ),
        in_specs=[hbm, hbm],
        out_specs=(hbm, hbm, hbm),
        scratch_shapes=[
            pltpu.VMEM((ROWS, WIDTH), BF),
            pltpu.VMEM((ROWS, 2 * HEAD), F32),
            pltpu.SemaphoreType.DMA((5,)),
            pltpu.SemaphoreType.DMA((6,)),
        ],
    )(input_grad, prompt_grads)


def body(
    queries,
    response_keys,
    response_values,
    prompt_key_rows,
    prompt_value_rows,
    upstream,
    lengths,
    query_weight,
    key_matrix,
    value_matrix,
    out_weight,
):
    vmem = pl.BlockSpec(memory_space=pltpu.VMEM)
    smem = pl.BlockSpec(memory_space=pltpu.SMEM)
    hbm = pl.BlockSpec(memory_space=pl.ANY)
    dma = pltpu.SemaphoreType.DMA
    input_grad, prompt_grads = pl.pallas_call(
        kernel,
        out_shape=(
            jax.ShapeDtypeStruct((1, ROWS, WIDTH), BF),
            jax.ShapeDtypeStruct((ROWS, 2 * HEAD), F32),
        ),
        in_specs=[smem] + [hbm] * 10,
        out_specs=(hbm, vmem),
        scratch_shapes=[
            pltpu.VMEM((8, ROWS, WIDTH), BF),
            pltpu.VMEM((HEADS * HEAD, WIDTH), BF),
            pltpu.VMEM((WIDTH, 896), BF),
            pltpu.VMEM((4, HEADS, SUB, HEAD), BF),
            pltpu.VMEM((24, ROWS, 2 * HEAD), BF),
            pltpu.VMEM((6, HEAD, CHUNK), BF),
            pltpu.VMEM((6, HEAD, CHUNK), BF),
            pltpu.VMEM((2, 6, CHUNK, LANES), F32),
            pltpu.VMEM((4, 6, CHUNK, LANES), BF),
            pltpu.VMEM((4, HEAD, LANES), F32),
            pltpu.VMEM((4 * SUB, HEADS * HEAD), F32),
            pltpu.VMEM((4, HEADS, SUB, HEAD), F32),
            pltpu.VMEM((4, HEADS, SUB, HEAD), BF),
            pltpu.VMEM((4, 8, LANES), F32),
            pltpu.VMEM((CHUNK, 2 * LANES), BF),
            pltpu.VMEM((HEAD, 2 * LANES), F32),
            pltpu.VMEM((24, ROWS, 2 * HEAD), F32),
            pltpu.VMEM((8 * ROWS, 896), BF),
            pltpu.VMEM((31, ROWS, QUARTER), BF),
            pltpu.VMEM((8, ROWS, 2 * HEAD), BF),
            pltpu.VMEM((8, ROWS, 2 * HEAD), BF),
            pltpu.VMEM((3, 2, ROWS, 2 * HEAD), BF),
            pltpu.VMEM((ROWS, 2 * HEAD), BF),
            dma((36,)),
            dma((4,)),
            dma((30,)),
            dma((30,)),
            dma((31,)),
            dma((31,)),
            dma((13,)),
            dma((13,)),
        ],
        compiler_params=pltpu.CompilerParams(
            collective_id=0, has_side_effects=True, vmem_limit_bytes=62 * 1024 * 1024
        ),
        cost_estimate=pl.CostEstimate(
            flops=18_000_000_000, bytes_accessed=20_000_000, transcendentals=4_000_000
        ),
    )(
        lengths,
        queries,
        response_keys,
        response_values,
        prompt_key_rows,
        prompt_value_rows,
        upstream,
        query_weight,
        key_matrix,
        value_matrix,
        out_weight,
    )
    return split(input_grad, prompt_grads)


def solution(mesh):
    in_specs = (
        P("resp", None, "tp"),
        P("resp", None, "tp"),
        P("resp", None, "tp"),
        P("resp", "tp"),
        P("resp", "tp"),
        P("resp", "tp", None),
        P("resp"),
        P(None, "tp"),
        P(None, "tp"),
        P(None, "tp"),
        P("tp", None),
    )
    out_specs = (P("resp", "tp", None), P("resp", "tp"), P("resp", "tp"))
    return jax.shard_map(body, mesh=mesh, in_specs=in_specs, out_specs=out_specs, check_vma=False)
```
